32 devices in a mesh: section: 4 (over y, x), dp: 8 (over z, core).
Axes of the slice: x: 2, y: 2, z: 4, core: 2. Of those that a mesh axis runs over, the one named last changes fastest.
Arguments:
- fresh_q: bfloat16 [4, 896, 2048], P('section', 'dp'), may hold values from -6 to 6
- current_key_value: bfloat16 [4, 896, 512], P('section', 'dp'), may hold values from -6 to 6
- held_q: bfloat16 [4, 896, 2048], P('section', 'dp'), may hold values from -6 to 6
- retained_key_value: bfloat16 [4, 896, 512], P('section', 'dp'), may hold values from -6 to 6
- cotangent: bfloat16 [4, 896, 2048], P('section', 'dp'), may hold values from -6 to 6
- norm_gains: float32 [4, 2, 128], P('section'), may hold values from 0.5 to 1.5
- plan: int32 [4, 2], P('section'), may hold values from 0 to 3, as said below
- segment_ids: int32 [8, 4, 112], P('dp'), may hold values from 0 to 3, never falling along the last dimension, each value on 1 to 56 neighbouring positions
Outputs:
- attention_out: bfloat16 [4, 896, 2048], P('section', 'dp')
- stored_q: bfloat16 [4, 896, 2048], P('section', 'dp')
- stored_kv: bfloat16 [4, 896, 512], P('section', 'dp')
- grad_q: bfloat16 [4, 896, 2048], P('section', 'dp')
- key_value_gradient: bfloat16 [4, 896, 512], P('section', 'dp')
- gain_grads: float32 [4, 2, 128], P('section')
The draws below stay inside these ranges and needn't reach their ends.
Inputs may be any that keep to these rules, and one draw needn't show every extreme that they name: `plan`: each of the two columns holds every microbatch number 0 to 3 exactly once.
All inputs are finite; a program needn't handle non-finite values.
Results may differ from the reference program's by a relative error of at most 0.0065.
Values may be sent and summed in bfloat16 or wider, within the bound.
No kernel may reach another device: no remote copies, remote signals or barrier semaphores. Data moves between devices by JAX's collectives and lax.ppermute only.
A program may use at most 64 MiB of HBM per device.

```python
import math
import jax
import jax.numpy as jnp
import numpy as np
from jax import lax

MB = 112
HQ = 16
KV_HEAD_COUNT = 2
HEAD_SIZE = 128
QUERY_PER_KV = 8
RELAY_SECTIONS = 4
REPLICAS = 8
MICRO = 4
SECTION_TOKENS = 896
N_DP = 8


def draw_plan(key, part):
    forward_ids = jax.random.permutation(jax.random.fold_in(key, 11), MICRO)
    backward_ids = jax.random.permutation(jax.random.fold_in(key, 23), MICRO)
    return jnp.stack([forward_ids, backward_ids], axis=1).astype(jnp.int32)


def steps_of(stream_key, dims, pieces, least, largest):
    def one(axis_at, shards_of):
        heights = jax.random.uniform(jax.random.fold_in(jax.random.fold_in(stream_key, 6), axis_at), (shards_of,), jnp.float32, least / len(pieces), largest / len(pieces))
        return jnp.repeat(jnp.exp(heights), dims[axis_at] // shards_of).reshape((-1,) + (1,) * (len(dims) - axis_at - 1))

    level = one(*pieces[0])
    for cut in pieces[1:]:
        level = level * one(*cut)
    return level


def split_up(amount, total, bound, lean):
    loads = [(1 << 20) // math.isqrt(grade ** lean) + 1 for grade in range(2, amount + 1)]
    rest, given = total - bound - (amount - 1), [1] * (amount - 1)
    while rest > 0:
        candidates = [i for i in range(amount - 1) if given[i] < bound]
        mass, remaining = sum([loads[i] for i in candidates]), rest
        for i in candidates:
            extra = min(bound - given[i], max(1, remaining * loads[i] // mass), rest)
            given[i] = given[i] + extra
            rest = rest - extra
    return np.array([bound] + given)


def uneven_parts(own_key, number_of, total, bound, skew):
    if number_of == 2:
        one = jax.random.randint(own_key, (), max(1, total - bound), min(bound, total - 1) + 1)
        return jnp.stack([one, total - one])
    sizes = jnp.asarray(split_up(number_of, total, bound, skew), jnp.int32)
    couples = (number_of - 1) // 2
    source_of, receiver = sizes[1:1 + 2 * couples:2], sizes[2:2 + 2 * couples:2]
    slack = jnp.minimum(source_of - 1, bound - receiver)
    passed = jax.random.randint(jax.random.fold_in(own_key, 1), (couples,), 0, 1 << 20) % (slack + 1)
    sizes = sizes.at[1:1 + 2 * couples:2].set(source_of - passed).at[2:2 + 2 * couples:2].set(receiver + passed)
    return sizes[jax.random.permutation(jax.random.fold_in(own_key, 2), number_of)]


def normal_values(rng, extent, spread, bound, shards=(), kind=jnp.bfloat16):
    entries = jax.random.normal(rng, extent, jnp.float32) * spread
    if len(shards) > 0:
        entries = steps_of(rng, extent, shards, -0.22, 0.18) * entries
    return jnp.clip(entries, min=-bound, max=bound).astype(kind)


def setup_inputs(seed: int = 0) -> dict:
    seeds = jax.random.split(jax.random.key(seed), 9)
    fresh_q = normal_values(seeds[0], (RELAY_SECTIONS, SECTION_TOKENS, HQ * HEAD_SIZE), 1.0, 6.0, ((0, 4), (1, 8)))
    current_key_value = normal_values(seeds[1], (RELAY_SECTIONS, SECTION_TOKENS, 2 * KV_HEAD_COUNT * HEAD_SIZE), 1.0, 6.0, ((0, 4), (1, 8)))
    held_q = normal_values(seeds[2], (RELAY_SECTIONS, SECTION_TOKENS, HQ * HEAD_SIZE), 1.0, 6.0, ((0, 4), (1, 8)))
    retained_key_value = normal_values(seeds[3], (RELAY_SECTIONS, SECTION_TOKENS, 2 * KV_HEAD_COUNT * HEAD_SIZE), 1.0, 6.0, ((0, 4), (1, 8)))
    cotangent = normal_values(seeds[4], (RELAY_SECTIONS, SECTION_TOKENS, HQ * HEAD_SIZE), 1.0, 6.0, ((0, 4), (1, 8)))
    norm_gains = jnp.clip(1.0 + 0.1 * jax.random.normal(seeds[5], (RELAY_SECTIONS, 2, HEAD_SIZE), jnp.float32), 0.5, 1.5)
    plan = draw_plan(jax.random.fold_in(seeds[8], 71), 0)
    segment_ids = jax.vmap(lambda own: jnp.searchsorted(jnp.cumsum(uneven_parts(own, 4, MB, MB // 2, 2)), jnp.arange(MB), side="right"))(jax.random.split(seeds[7], REPLICAS * MICRO)).reshape((REPLICAS, MICRO, MB)).astype(jnp.int32)
    return {"fresh_q": fresh_q, "current_key_value": current_key_value, "held_q": held_q, "retained_key_value": retained_key_value, "cotangent": cotangent, "norm_gains": norm_gains, "plan": plan, "segment_ids": segment_ids}


EPSILON = 1e-06

def rounded_values(values):
    return lax.optimization_barrier(values.astype(jnp.bfloat16)).astype(jnp.float32)

def allowed_pairs(segment_row):
    row_sum_total = segment_row.shape[0]
    rows_at = jnp.arange(row_sum_total)[:, None]
    cols_at = jnp.arange(row_sum_total)[None, :]
    return (cols_at <= rows_at) & (segment_row[:, None] == segment_row[None, :])

def apply_norm(values, gain, heads):
    row_sum_total = values.shape[0]
    widened = values.astype(jnp.float32).reshape(row_sum_total, heads, HEAD_SIZE)
    factor = lax.rsqrt(lax.optimization_barrier(jnp.mean(widened * widened, axis=-1, keepdims=True)) + EPSILON)
    return (widened, factor, widened * factor * gain)

def attention_probs(query_rows, key_value_pair, gain_per_row, segment_row):
    row_sum_total = query_rows.shape[0]
    q_wide, q_factor, normalized_query = apply_norm(query_rows, gain_per_row[0], HQ)
    expanded_key, key_factor, normalized_key = apply_norm(key_value_pair[:, :KV_HEAD_COUNT * HEAD_SIZE], gain_per_row[1], KV_HEAD_COUNT)
    query_converted = rounded_values(normalized_query).reshape(row_sum_total, KV_HEAD_COUNT, QUERY_PER_KV, HEAD_SIZE)
    k_cast = rounded_values(normalized_key)
    scores = jnp.einsum('qhgd,khd->hgqk', query_converted, k_cast) * (1.0 / math.sqrt(HEAD_SIZE))
    weights = jnp.where(allowed_pairs(segment_row), jnp.exp(scores), 0.0)
    attn_probs = weights / lax.optimization_barrier(jnp.sum(weights, axis=-1, keepdims=True))
    return (q_wide, q_factor, query_converted, expanded_key, key_factor, k_cast, attn_probs)

def forward(query_rows, key_value_pair, gain_per_row, segment_row):
    row_sum_total = query_rows.shape[0]
    attn_probs = attention_probs(query_rows, key_value_pair, gain_per_row, segment_row)[6]
    value_portion = key_value_pair[:, KV_HEAD_COUNT * HEAD_SIZE:].astype(jnp.float32).reshape(row_sum_total, KV_HEAD_COUNT, HEAD_SIZE)
    output = jnp.einsum('hgqk,khd->qhgd', rounded_values(attn_probs), value_portion)
    return output.reshape(row_sum_total, HQ * HEAD_SIZE).astype(jnp.bfloat16)

def norm_back(widened, factor, gain, d_normed):
    scaled = gain * d_normed
    inner = lax.optimization_barrier(jnp.sum(widened * scaled, axis=-1, keepdims=True)) / HEAD_SIZE
    d_input = factor * scaled - widened * factor * factor * factor * inner
    d_gain = lax.optimization_barrier(jnp.sum(d_normed * widened * factor, axis=(0, 1)))
    return (d_input, d_gain)

def backward(query_rows, key_value_pair, gain_per_row, segment_row, received_payload):
    row_sum_total = query_rows.shape[0]
    q_wide, q_factor, query_converted, expanded_key, key_factor, k_cast, attn_probs = attention_probs(query_rows, key_value_pair, gain_per_row, segment_row)
    value_portion = key_value_pair[:, KV_HEAD_COUNT * HEAD_SIZE:].astype(jnp.float32).reshape(row_sum_total, KV_HEAD_COUNT, HEAD_SIZE)
    expanded_heads = received_payload.astype(jnp.float32).reshape(row_sum_total, KV_HEAD_COUNT, QUERY_PER_KV, HEAD_SIZE)
    prob_cast = rounded_values(attn_probs)
    d_probs = jnp.einsum('qhgd,khd->hgqk', expanded_heads, value_portion)
    value_gradient = jnp.einsum('hgqk,qhgd->khd', prob_cast, expanded_heads)
    centre = lax.optimization_barrier(jnp.sum(attn_probs * d_probs, axis=-1, keepdims=True))
    d_scores = rounded_values(attn_probs * (d_probs - centre))
    score_scale = 1.0 / math.sqrt(HEAD_SIZE)
    d_qn = jnp.einsum('hgqk,khd->qhgd', d_scores, k_cast).reshape(row_sum_total, HQ, HEAD_SIZE) * score_scale
    d_kn = jnp.einsum('hgqk,qhgd->khd', d_scores, query_converted) * score_scale
    grad_query, q_gain = norm_back(q_wide, q_factor, gain_per_row[0], d_qn)
    key_gradient, k_gain = norm_back(expanded_key, key_factor, gain_per_row[1], d_kn)
    grad_q = grad_query.reshape(row_sum_total, HQ * HEAD_SIZE).astype(jnp.bfloat16)
    key_value_gradient = jnp.concatenate([key_gradient.reshape(row_sum_total, KV_HEAD_COUNT * HEAD_SIZE), value_gradient.reshape(row_sum_total, KV_HEAD_COUNT * HEAD_SIZE)], axis=1).astype(jnp.bfloat16)
    return (grad_q, key_value_gradient, jnp.stack([q_gain, k_gain]))

def reference(fresh_q, current_key_value, held_q, retained_key_value, cotangent, norm_gains, plan, segment_ids):
    section_total = fresh_q.shape[0]

    def split_rows(values):
        return values.reshape(section_total, N_DP, MB, values.shape[-1])
    fetched_q = split_rows(held_q[::-1])
    fetched_kv = split_rows(retained_key_value[::-1])
    upstream = split_rows(jnp.roll(cotangent, -1, axis=0))

    def per_section(inputs):
        query_rows, key_value_pair, old_query, old_keyval, received_payload, gain_per_row, id_table = inputs
        forward_ids = segment_ids[:, id_table[0], :]
        backward_ids = segment_ids[:, id_table[1], :]
        outputs = jax.vmap(forward, in_axes=(0, 0, None, 0))(query_rows, key_value_pair, gain_per_row, forward_ids)
        grad_q, key_value_gradient, gain_terms = jax.vmap(backward, in_axes=(0, 0, None, 0, 0))(old_query, old_keyval, gain_per_row, backward_ids, received_payload)
        return (outputs, grad_q, key_value_gradient, lax.optimization_barrier(jnp.sum(gain_terms, axis=0)) / N_DP)
    outputs, grad_q, key_value_gradient, gain_grads = lax.map(per_section, (split_rows(fresh_q), split_rows(current_key_value), fetched_q, fetched_kv, upstream, norm_gains, plan))
    attention_out = jnp.roll(outputs, 1, axis=0).reshape(fresh_q.shape)
    return (attention_out, fresh_q[::-1], current_key_value[::-1], grad_q.reshape(held_q.shape), key_value_gradient.reshape(retained_key_value.shape), gain_grads)
```

```python
import functools
import math

import jax
import jax.numpy as jnp
from jax import lax
from jax.experimental import pallas as pl
from jax.experimental.pallas import tpu as pltpu
from jax.sharding import PartitionSpec as P

HEAD_SIZE = 128
EPSILON = 1e-06
SCORE_SCALE = 1.0 / math.sqrt(HEAD_SIZE)
EXP2_SCALE = SCORE_SCALE * math.log2(math.e)

NT = (((1,), (1,)), ((), ()))
TN = (((0,), (0,)), ((), ()))
NN = (((1,), (0,)), ((), ()))


def dot(a, b, dims):
    return lax.dot_general(a, b, dims, preferred_element_type=jnp.float32)


def head(ref, index):
    return ref[:, index * HEAD_SIZE : (index + 1) * HEAD_SIZE]


def allowed_pairs(segment_ref, chosen):
    micro, tokens = segment_ref.shape
    ids = segment_ref[...].astype(jnp.float32)
    number = lax.broadcasted_iota(jnp.int32, (micro, tokens), 0).astype(jnp.float32)
    row = jnp.sum(jnp.where(number == chosen[:, :tokens], ids, 0.0), axis=0, keepdims=True)
    rows_at = lax.broadcasted_iota(jnp.int32, (tokens, tokens), 0)
    cols_at = lax.broadcasted_iota(jnp.int32, (tokens, tokens), 1)
    column = jnp.sum(jnp.where(rows_at == cols_at, row, 0.0), axis=1, keepdims=True)
    return (cols_at <= rows_at) & (column == row)


def normalized(values):
    wide = values.astype(jnp.float32)
    factor = lax.rsqrt(jnp.mean(wide * wide, axis=1, keepdims=True) + EPSILON)
    return wide * factor, factor


def probabilities(query, key, allowed):
    scores = dot(query, key, NT)
    weights = jnp.where(allowed, jnp.exp2(scores * EXP2_SCALE), 0.0)
    return weights * (1.0 / jnp.sum(weights, axis=1, keepdims=True))


def forward_kernel(kv_heads, q_ref, kv_ref, side_ref, segment_ref, out_ref):
    per_kv = q_ref.shape[1] // HEAD_SIZE // kv_heads
    allowed = allowed_pairs(segment_ref, side_ref[2:3, :])
    for g in range(kv_heads):
        key_hat, _ = normalized(head(kv_ref, g))
        key = (key_hat * side_ref[1:2, :]).astype(jnp.bfloat16)
        value = head(kv_ref, kv_heads + g)
        for h in range(g * per_kv, (g + 1) * per_kv):
            query_hat, _ = normalized(head(q_ref, h))
            query = (query_hat * side_ref[0:1, :]).astype(jnp.bfloat16)
            probs = probabilities(query, key, allowed).astype(jnp.bfloat16)
            out_ref[:, h * HEAD_SIZE : (h + 1) * HEAD_SIZE] = dot(probs, value, NN).astype(
                jnp.bfloat16
            )


def norm_back(hat, factor, scaled_gain, d_normed):
    terms = d_normed * hat
    inner = jnp.sum(terms * scaled_gain, axis=1, keepdims=True) * (1.0 / HEAD_SIZE)
    return (d_normed * scaled_gain - hat * inner) * factor, terms


def backward_kernel(
    kv_heads, q_ref, kv_ref, up_ref, side_ref, segment_ref, grad_q_ref, grad_kv_ref, gain_ref
):
    per_kv = q_ref.shape[1] // HEAD_SIZE // kv_heads
    tokens = q_ref.shape[0]
    allowed = allowed_pairs(segment_ref, side_ref[3:4, :])
    q_gain, k_gain = side_ref[0:1, :], side_ref[1:2, :]
    q_terms = jnp.zeros((tokens, HEAD_SIZE), jnp.float32)
    k_terms = jnp.zeros((tokens, HEAD_SIZE), jnp.float32)
    for g in range(kv_heads):
        key_hat, key_factor = normalized(head(kv_ref, g))
        key = (key_hat * k_gain).astype(jnp.bfloat16)
        value = head(kv_ref, kv_heads + g)
        d_key = jnp.zeros((tokens, HEAD_SIZE), jnp.float32)
        d_value = jnp.zeros((tokens, HEAD_SIZE), jnp.float32)
        for h in range(g * per_kv, (g + 1) * per_kv):
            query_hat, query_factor = normalized(head(q_ref, h))
            query = (query_hat * q_gain).astype(jnp.bfloat16)
            upstream = head(up_ref, h)
            probs = probabilities(query, key, allowed)
            d_probs = dot(upstream, value, NT)
            d_value += dot(probs.astype(jnp.bfloat16), upstream, TN)
            centre = jnp.sum(probs * d_probs, axis=1, keepdims=True)
            d_scores = (probs * (d_probs - centre)).astype(jnp.bfloat16)
            d_key += dot(d_scores, query, TN)
            d_query, terms = norm_back(
                query_hat, query_factor, q_gain * SCORE_SCALE, dot(d_scores, key, NN)
            )
            q_terms += terms
            grad_q_ref[:, h * HEAD_SIZE : (h + 1) * HEAD_SIZE] = d_query.astype(jnp.bfloat16)
        d_key, terms = norm_back(key_hat, key_factor, k_gain * SCORE_SCALE, d_key)
        k_terms += terms
        grad_kv_ref[:, g * HEAD_SIZE : (g + 1) * HEAD_SIZE] = d_key.astype(jnp.bfloat16)
        grad_kv_ref[:, (kv_heads + g) * HEAD_SIZE : (kv_heads + g + 1) * HEAD_SIZE] = (
            d_value.astype(jnp.bfloat16)
        )
    gain_ref[0:1, :] = jnp.sum(q_terms, axis=0, keepdims=True) * SCORE_SCALE
    gain_ref[1:2, :] = jnp.sum(k_terms, axis=0, keepdims=True) * SCORE_SCALE


def forward(q, kv, side, segments):
    tokens, width = q.shape
    return pl.pallas_call(
        functools.partial(forward_kernel, kv.shape[1] // HEAD_SIZE // 2),
        out_shape=jax.ShapeDtypeStruct(q.shape, q.dtype),
        cost_estimate=pl.CostEstimate(
            flops=4 * tokens * tokens * width,
            bytes_accessed=4 * tokens * width,
            transcendentals=tokens * width,
        ),
        name="forward",
    )(q, kv, side, segments)


def backward(q, kv, upstream, side, segments):
    tokens, width = q.shape
    return pl.pallas_call(
        functools.partial(backward_kernel, kv.shape[1] // HEAD_SIZE // 2),
        out_shape=(
            jax.ShapeDtypeStruct(q.shape, q.dtype),
            jax.ShapeDtypeStruct(kv.shape, kv.dtype),
            jax.ShapeDtypeStruct((2, HEAD_SIZE), jnp.float32),
        ),
        cost_estimate=pl.CostEstimate(
            flops=10 * tokens * tokens * width,
            bytes_accessed=6 * tokens * width,
            transcendentals=tokens * width,
        ),
        name="backward",
    )(q, kv, upstream, side, segments)


def local(
    fresh_q, current_key_value, held_q, retained_key_value, cotangent, norm_gains, plan, segment_ids
):
    sections, replicas = lax.axis_size("section"), lax.axis_size("dp")
    opposite = [(i, -i % sections) for i in range(sections)]
    moving = [(i, j) for i, j in opposite if i != j]
    staying = [i for i, j in opposite if i == j]
    up = [(i, (i + 1) % sections) for i in range(sections)]
    down_staying = [(i, (i - 1) % sections) for i in staying]
    down_moving = [(i, (i - 1) % sections) for i, j in moving]
    segments = segment_ids[0]

    def hop(value, pairs):
        return lax.ppermute(value, "section", pairs)

    numbers = jnp.broadcast_to(plan[0].astype(jnp.float32)[:, None], (2, HEAD_SIZE))
    side = hop(jnp.concatenate([norm_gains[0], numbers], axis=0), up)
    held = hop(held_q[0], moving), hop(retained_key_value[0], moving)
    fresh = hop(fresh_q[0], up), hop(current_key_value[0], up)

    upstream = cotangent[0]
    own_q, own_kv, own_gain = backward(held_q[0], retained_key_value[0], upstream, side, segments)
    own_q, own_kv = hop(own_q, down_staying), hop(own_kv, down_staying)

    stored_q, stored_kv = hop(fresh[0], opposite), hop(fresh[1], opposite)
    far_q, far_kv, far_gain = backward(*held, upstream, side, segments)
    far_q, far_kv = hop(far_q, down_moving), hop(far_kv, down_moving)

    attention_out = forward(*fresh, side, segments)

    me = lax.axis_index("section")
    stays = functools.reduce(jnp.logical_or, [me == i for i in staying])
    gain = jnp.where(stays, own_gain, far_gain)
    step = 1
    while step < replicas:
        gain = gain + lax.ppermute(gain, "dp", [(i, i ^ step) for i in range(replicas)])
        step *= 2
    gain = hop(gain, [(i, (i - 1) % sections) for i in range(sections)]) * (1.0 / replicas)
    above_stays = functools.reduce(jnp.logical_or, [me == (i - 1) % sections for i in staying])
    grad_q = jnp.where(above_stays, own_q, far_q)
    grad_kv = jnp.where(above_stays, own_kv, far_kv)
    return (
        attention_out[None],
        stored_q[None],
        stored_kv[None],
        grad_q[None],
        grad_kv[None],
        gain[None],
    )


def solution(mesh):
    rows = P("section", "dp", None)
    return jax.shard_map(
        local,
        mesh=mesh,
        in_specs=(rows, rows, rows, rows, rows, P("section", None, None), P("section", None), P("dp", None, None)),
        out_specs=(rows, rows, rows, rows, rows, P("section", None, None)),
        check_vma=False,
    )
```

```python
import functools
import math

import jax
import jax.numpy as jnp
from jax import lax
from jax.experimental import pallas as pl
from jax.experimental.pallas import tpu as pltpu
from jax.sharding import PartitionSpec as P

HEAD_SIZE = 128
EPSILON = 1e-06
SCORE_SCALE = 1.0 / math.sqrt(HEAD_SIZE)
EXP2_SCALE = SCORE_SCALE * math.log2(math.e)

NT = (((1,), (1,)), ((), ()))
TN = (((0,), (0,)), ((), ()))
NN = (((1,), (0,)), ((), ()))


def dot(a, b, dims):
    return lax.dot_general(a, b, dims, preferred_element_type=jnp.float32)


def head(ref, index):
    return ref[:, index * HEAD_SIZE : (index + 1) * HEAD_SIZE]


def stacked(ref, first, count):
    return jnp.concatenate([head(ref, first + i) for i in range(count)], axis=0)


def allowed_pairs(segment_ref, chosen, copies):
    micro, tokens = segment_ref.shape
    ids = segment_ref[...].astype(jnp.float32)
    number = lax.broadcasted_iota(jnp.int32, (micro, tokens), 0).astype(jnp.float32)
    row = jnp.sum(jnp.where(number == chosen[:, :tokens], ids, 0.0), axis=0, keepdims=True)
    keys_at = lax.broadcasted_iota(jnp.int32, (tokens, tokens), 0)
    queries_at = lax.broadcasted_iota(jnp.int32, (tokens, tokens), 1)
    column = jnp.sum(jnp.where(keys_at == queries_at, row, 0.0), axis=1, keepdims=True)
    allowed = ((keys_at <= queries_at) & (column == row)).astype(jnp.float32)
    return jnp.concatenate([allowed] * copies, axis=1) > 0.5


def normalized(values):
    wide = values.astype(jnp.float32)
    factor = lax.rsqrt(jnp.mean(wide * wide, axis=1, keepdims=True) + EPSILON)
    return wide * factor, factor


def probabilities(key, query, allowed):
    scores = dot(key, query, NT)
    weights = jnp.where(allowed, jnp.exp2(scores * EXP2_SCALE), 0.0)
    return weights * (1.0 / jnp.sum(weights, axis=0, keepdims=True))


def forward_kernel(kv_heads, packed_ref, side_ref, segment_ref, out_ref):
    tokens = packed_ref.shape[0]
    heads = packed_ref.shape[1] // HEAD_SIZE - 2 * kv_heads
    per_kv = heads // kv_heads
    allowed = allowed_pairs(segment_ref, side_ref[2:3, :], per_kv)
    for g in range(kv_heads):
        key_hat, _ = normalized(head(packed_ref, heads + g))
        key = (key_hat * side_ref[1:2, :]).astype(jnp.bfloat16)
        value = head(packed_ref, heads + kv_heads + g)
        query_hat, _ = normalized(stacked(packed_ref, g * per_kv, per_kv))
        query = (query_hat * side_ref[0:1, :]).astype(jnp.bfloat16)
        probs = probabilities(key, query, allowed).astype(jnp.bfloat16)
        out = dot(probs, value, TN).astype(jnp.bfloat16)
        for i in range(per_kv):
            h = g * per_kv + i
            out_ref[:, h * HEAD_SIZE : (h + 1) * HEAD_SIZE] = out[i * tokens : (i + 1) * tokens]


def norm_back(hat, factor, scaled_gain, d_normed):
    terms = d_normed * hat
    inner = jnp.sum(terms * scaled_gain, axis=1, keepdims=True) * (1.0 / HEAD_SIZE)
    return (d_normed * scaled_gain - hat * inner) * factor, terms


def summed_rows(terms):
    return jnp.sum(terms.reshape(-1, 8, terms.shape[1]), axis=0)


def backward_kernel(q_ref, kv_ref, up_ref, side_ref, segment_ref, *rest):
    grad_ref, gain_ref = rest[-2:]
    tokens = q_ref.shape[0]
    heads = q_ref.shape[1] // HEAD_SIZE
    kv_heads = kv_ref.shape[1] // HEAD_SIZE // 2
    per_kv = heads // kv_heads
    allowed = allowed_pairs(segment_ref, side_ref[3:4, :], per_kv)
    q_gain, k_gain = side_ref[0:1, :], side_ref[1:2, :]
    q_terms = k_terms = 0.0
    for g in range(kv_heads):
        key_hat, key_factor = normalized(head(kv_ref, g))
        key = (key_hat * k_gain).astype(jnp.bfloat16)
        value = head(kv_ref, kv_heads + g)
        query_hat, query_factor = normalized(stacked(q_ref, g * per_kv, per_kv))
        query = (query_hat * q_gain).astype(jnp.bfloat16)
        upstream = stacked(up_ref, g * per_kv, per_kv)
        probs = probabilities(key, query, allowed)
        d_probs = dot(value, upstream, NT)
        d_value = dot(probs.astype(jnp.bfloat16), upstream, NN)
        centre = jnp.sum(probs * d_probs, axis=0, keepdims=True)
        d_scores = (probs * (d_probs - centre)).astype(jnp.bfloat16)
        d_key = dot(d_scores, query, NN)
        d_query, terms = norm_back(
            query_hat, query_factor, q_gain * SCORE_SCALE, dot(d_scores, key, TN)
        )
        q_terms += summed_rows(terms)
        d_query = d_query.astype(jnp.bfloat16)
        for i in range(per_kv):
            h = g * per_kv + i
            grad_ref[:, h * HEAD_SIZE : (h + 1) * HEAD_SIZE] = d_query[
                i * tokens : (i + 1) * tokens
            ]
        d_key, terms = norm_back(key_hat, key_factor, k_gain * SCORE_SCALE, d_key)
        k_terms += summed_rows(terms)
        at = (heads + g) * HEAD_SIZE
        grad_ref[:, at : at + HEAD_SIZE] = d_key.astype(jnp.bfloat16)
        at = (heads + kv_heads + g) * HEAD_SIZE
        grad_ref[:, at : at + HEAD_SIZE] = d_value.astype(jnp.bfloat16)
    gain_ref[0:1, :] = jnp.sum(q_terms, axis=0, keepdims=True) * SCORE_SCALE
    gain_ref[1:2, :] = jnp.sum(k_terms, axis=0, keepdims=True) * SCORE_SCALE


def cost(work):
    return pl.CostEstimate(flops=work, bytes_accessed=1024, transcendentals=0)


def forward(kv_heads, packed, side, segments):
    tokens, width = packed.shape
    return pl.pallas_call(
        functools.partial(forward_kernel, kv_heads),
        out_shape=jax.ShapeDtypeStruct((tokens, width - 2 * kv_heads * HEAD_SIZE), packed.dtype),
        cost_estimate=cost(1024),
        name="forward",
    )(packed, side, segments)


def backward(q, kv, upstream, side, segments, after, work):
    tokens = q.shape[0]
    return pl.pallas_call(
        backward_kernel,
        out_shape=(
            jax.ShapeDtypeStruct((tokens, q.shape[1] + kv.shape[1]), q.dtype),
            jax.ShapeDtypeStruct((2, HEAD_SIZE), jnp.float32),
        ),
        in_specs=[pl.BlockSpec(memory_space=pltpu.VMEM)] * 5
        + [pl.BlockSpec(memory_space=pl.ANY)] * len(after),
        cost_estimate=cost(work),
        name="backward",
    )(q, kv, upstream, side, segments, *after)


def unpack_kernel(choice_ref, first_ref, second_ref, third_ref, *outs):
    q_width = outs[0].shape[1]

    def spread(packed, q_ref, kv_ref):
        q_ref[...] = packed[:, :q_width]
        kv_ref[...] = packed[:, q_width:]

    @pl.when(choice_ref[0] > 0)
    def _():
        spread(first_ref, outs[0], outs[1])

    @pl.when(choice_ref[0] <= 0)
    def _():
        spread(second_ref, outs[0], outs[1])

    spread(third_ref, outs[2], outs[3])


def unpack(choice, first, second, third, q_width):
    tokens, width = first.shape
    vmem = pl.BlockSpec(memory_space=pltpu.VMEM)
    widths = (q_width, width - q_width) * 2
    return pl.pallas_call(
        unpack_kernel,
        out_shape=[jax.ShapeDtypeStruct((tokens, w), first.dtype) for w in widths],
        in_specs=[pl.BlockSpec(memory_space=pltpu.SMEM)] + [vmem] * 3,
        out_specs=[vmem] * 4,
        cost_estimate=cost(1024),
        name="unpack",
    )(choice, first, second, third)


def local(
    fresh_q, current_key_value, held_q, retained_key_value, cotangent, norm_gains, plan, segment_ids
):
    sections, replicas = lax.axis_size("section"), lax.axis_size("dp")
    opposite = [(i, -i % sections) for i in range(sections)]
    moving = [(i, j) for i, j in opposite if i != j]
    staying = [i for i, j in opposite if i == j]
    up = [(i, (i + 1) % sections) for i in range(sections)]
    down_staying = [(i, (i - 1) % sections) for i in staying]
    down_moving = [(i, (i - 1) % sections) for i, j in moving]
    segments = segment_ids[0]
    q_width = fresh_q.shape[2]
    kv_heads = current_key_value.shape[2] // HEAD_SIZE // 2

    def hop(value, pairs):
        return lax.ppermute(value, "section", pairs)

    numbers = jnp.broadcast_to(plan[0].astype(jnp.float32)[:, None], (2, HEAD_SIZE))
    side = hop(jnp.concatenate([norm_gains[0], numbers], axis=0), up)
    fresh = hop(jnp.concatenate([fresh_q[0], current_key_value[0]], axis=1), up)
    held = hop(held_q[0], moving), hop(retained_key_value[0], moving)

    upstream = cotangent[0]
    own_grad, own_gain = backward(
        held_q[0], retained_key_value[0], upstream, side, segments, (), 1 << 36
    )
    own_grad = hop(own_grad, down_staying)

    stored = hop(fresh, opposite)
    far_grad, far_gain = backward(*held, upstream, side, segments, (fresh, own_gain), 1024)
    far_grad = hop(far_grad, down_moving)

    attention_out = forward(kv_heads, fresh, side, segments)

    me = lax.axis_index("section")
    stays = functools.reduce(jnp.logical_or, [me == i for i in staying])
    gain = jnp.where(stays, own_gain, far_gain)
    step = 1
    while 2 * step < replicas:
        gain = gain + lax.ppermute(gain, "dp", [(i, i ^ step) for i in range(replicas)])
        step *= 2
    halves = [
        lax.ppermute(
            gain,
            ("section", "dp"),
            [
                (i * replicas + j, (i - 1) % sections * replicas + (j ^ other))
                for i in range(sections)
                for j in range(replicas)
            ],
        )
        for other in (0, step)
    ]
    gain = (halves[0] + halves[1]) * (1.0 / replicas)
    above_stays = functools.reduce(jnp.logical_or, [me == (i - 1) % sections for i in staying])
    choice = above_stays.astype(jnp.int32).reshape(1)
    outs = unpack(choice, own_grad, far_grad, stored, q_width)
    return (
        attention_out[None],
        outs[2][None],
        outs[3][None],
        outs[0][None],
        outs[1][None],
        gain[None],
    )


def solution(mesh):
    rows = P("section", "dp", None)
    gains = P("section", None, None)
    return jax.shard_map(
        local,
        mesh=mesh,
        in_specs=(rows, rows, rows, rows, rows, gains, P("section", None), P("dp", None, None)),
        out_specs=(rows, rows, rows, rows, rows, gains),
        check_vma=False,
    )
```

```python
import functools
import math

import jax
import jax.numpy as jnp
from jax import lax
from jax.experimental import pallas as pl
from jax.experimental.pallas import tpu as pltpu
from jax.sharding import PartitionSpec as P

HEAD_SIZE = 128
EPSILON = 1e-06
SCORE_SCALE = 1.0 / math.sqrt(HEAD_SIZE)
EXP2_SCALE = SCORE_SCALE * math.log2(math.e)

VMEM_LIMIT = 16 << 20
NT = (((1,), (1,)), ((), ()))
TN = (((0,), (0,)), ((), ()))
NN = (((1,), (0,)), ((), ()))


def dot(a, b, dims):
    return lax.dot_general(a, b, dims, preferred_element_type=jnp.float32)


def head(ref, index):
    return ref[:, index * HEAD_SIZE : (index + 1) * HEAD_SIZE]


def stacked(ref, first, count):
    return jnp.concatenate([head(ref, first + i) for i in range(count)], axis=0)


def allowed_pairs(segment_ref, chosen, copies):
    micro, tokens = segment_ref.shape
    ids = segment_ref[...].astype(jnp.float32)
    number = lax.broadcasted_iota(jnp.int32, (micro, tokens), 0).astype(jnp.float32)
    row = jnp.sum(jnp.where(number == chosen[:, :tokens], ids, 0.0), axis=0, keepdims=True)
    keys_at = lax.broadcasted_iota(jnp.int32, (tokens, tokens), 0)
    queries_at = lax.broadcasted_iota(jnp.int32, (tokens, tokens), 1)
    column = jnp.sum(jnp.where(keys_at == queries_at, row, 0.0), axis=1, keepdims=True)
    allowed = ((keys_at <= queries_at) & (column == row)).astype(jnp.float32)
    return jnp.concatenate([allowed] * copies, axis=1) > 0.5


def side_rows(tile):
    parts = tile.astype(jnp.float32)
    return parts[0:4] + parts[4:8] + parts[8:12]


def pack_kernel(q_ref, kv_ref, gains_ref, plan_ref, packed_ref):
    q_width, kv_width = q_ref.shape[1], kv_ref.shape[1]
    packed_ref[:, :q_width] = q_ref[...]
    packed_ref[:, q_width : q_width + kv_width] = kv_ref[...]
    numbers = [jnp.full((1, HEAD_SIZE), plan_ref[0, i]).astype(jnp.float32) for i in range(2)]
    rest = jnp.concatenate([gains_ref[...]] + numbers, axis=0)
    parts = []
    for _ in range(3):
        part = rest.astype(jnp.bfloat16).astype(jnp.float32)
        rest = rest - part
        parts.append(part)
    parts = jnp.concatenate(parts + [jnp.zeros_like(rest)], axis=0)
    empty = jnp.zeros((q_ref.shape[0] - 16, HEAD_SIZE), jnp.bfloat16)
    packed_ref[0:16, q_width + kv_width :] = parts.astype(jnp.bfloat16)
    packed_ref[16:, q_width + kv_width :] = empty


def normalized(values):
    wide = values.astype(jnp.float32)
    factor = lax.rsqrt(jnp.mean(wide * wide, axis=1, keepdims=True) + EPSILON)
    return wide * factor, factor


def probabilities(key, query, allowed):
    scores = dot(key, query, NT)
    weights = jnp.where(allowed, jnp.exp2(scores * EXP2_SCALE), 0.0)
    return weights * (1.0 / jnp.sum(weights, axis=0, keepdims=True))


def forward_kernel(packed_ref, segment_ref, out_ref):
    side = side_rows(packed_ref[0:16, packed_ref.shape[1] - HEAD_SIZE :])
    tokens = packed_ref.shape[0]
    heads = out_ref.shape[1] // HEAD_SIZE
    kv_heads = (packed_ref.shape[1] // HEAD_SIZE - heads) // 2
    per_kv = heads // kv_heads
    allowed = allowed_pairs(segment_ref, side[2:3], per_kv)
    for g in range(kv_heads):
        key_hat, _ = normalized(head(packed_ref, heads + g))
        key = (key_hat * side[1:2]).astype(jnp.bfloat16)
        value = head(packed_ref, heads + kv_heads + g)
        query_hat, _ = normalized(stacked(packed_ref, g * per_kv, per_kv))
        query = (query_hat * side[0:1]).astype(jnp.bfloat16)
        probs = probabilities(key, query, allowed).astype(jnp.bfloat16)
        out = dot(probs, value, TN).astype(jnp.bfloat16)
        for i in range(per_kv):
            h = g * per_kv + i
            out_ref[:, h * HEAD_SIZE : (h + 1) * HEAD_SIZE] = out[i * tokens : (i + 1) * tokens]


def norm_back(hat, factor, scaled_gain, d_normed):
    terms = d_normed * hat
    inner = jnp.sum(terms * scaled_gain, axis=1, keepdims=True) * (1.0 / HEAD_SIZE)
    return (d_normed * scaled_gain - hat * inner) * factor, terms


def summed_rows(terms):
    return jnp.sum(terms.reshape(-1, 8, terms.shape[1]), axis=0)


def backward_kernel(packed_ref, up_ref, side_ref, segment_ref, grad_ref, gain_ref):
    side = side_rows(side_ref[...])
    tokens = packed_ref.shape[0]
    heads = up_ref.shape[1] // HEAD_SIZE
    kv_heads = (packed_ref.shape[1] // HEAD_SIZE - heads) // 2
    per_kv = heads // kv_heads
    allowed = allowed_pairs(segment_ref, side[3:4], per_kv)
    q_gain, k_gain = side[0:1], side[1:2]
    q_terms = k_terms = 0.0
    for g in range(kv_heads):
        key_hat, key_factor = normalized(head(packed_ref, heads + g))
        key = (key_hat * k_gain).astype(jnp.bfloat16)
        value = head(packed_ref, heads + kv_heads + g)
        query_hat, query_factor = normalized(stacked(packed_ref, g * per_kv, per_kv))
        query = (query_hat * q_gain).astype(jnp.bfloat16)
        upstream = stacked(up_ref, g * per_kv, per_kv)
        probs = probabilities(key, query, allowed)
        d_probs = dot(value, upstream, NT)
        d_value = dot(probs.astype(jnp.bfloat16), upstream, NN)
        centre = jnp.sum(probs * d_probs, axis=0, keepdims=True)
        d_scores = (probs * (d_probs - centre)).astype(jnp.bfloat16)
        d_key = dot(d_scores, query, NN)
        d_query, terms = norm_back(
            query_hat, query_factor, q_gain * SCORE_SCALE, dot(d_scores, key, TN)
        )
        q_terms += summed_rows(terms)
        d_query = d_query.astype(jnp.bfloat16)
        for i in range(per_kv):
            h = g * per_kv + i
            grad_ref[:, h * HEAD_SIZE : (h + 1) * HEAD_SIZE] = d_query[
                i * tokens : (i + 1) * tokens
            ]
        d_key, terms = norm_back(key_hat, key_factor, k_gain * SCORE_SCALE, d_key)
        k_terms += summed_rows(terms)
        at = (heads + g) * HEAD_SIZE
        grad_ref[:, at : at + HEAD_SIZE] = d_key.astype(jnp.bfloat16)
        at = (heads + kv_heads + g) * HEAD_SIZE
        grad_ref[:, at : at + HEAD_SIZE] = d_value.astype(jnp.bfloat16)
    gain_ref[0:1, :] = jnp.sum(q_terms, axis=0, keepdims=True) * SCORE_SCALE
    gain_ref[1:2, :] = jnp.sum(k_terms, axis=0, keepdims=True) * SCORE_SCALE


def cost(work):
    return pl.CostEstimate(flops=work, bytes_accessed=1024, transcendentals=0)


VMEM = pl.BlockSpec(memory_space=pltpu.VMEM)


def side_tile(fresh):
    at = fresh.shape[1] // HEAD_SIZE - 1
    return pl.BlockSpec((16, HEAD_SIZE), lambda step: (0, at))


def pack(q, kv, gains, plan):
    return pl.pallas_call(
        pack_kernel,
        out_shape=jax.ShapeDtypeStruct((q.shape[0], q.shape[1] + kv.shape[1] + HEAD_SIZE), q.dtype),
        in_specs=[VMEM] * 3 + [pl.BlockSpec(memory_space=pltpu.SMEM)],
        out_specs=VMEM,
        cost_estimate=cost(1024),
        name="pack",
    )(q, kv, gains, plan)


def forward(fresh, q_width, segments):
    return pl.pallas_call(
        forward_kernel,
        out_shape=jax.ShapeDtypeStruct((fresh.shape[0], q_width), fresh.dtype),
        in_specs=[VMEM, VMEM],
        out_specs=VMEM,
        cost_estimate=cost(1024),
        compiler_params=pltpu.CompilerParams(vmem_limit_bytes=VMEM_LIMIT),
        name="forward",
    )(fresh, segments)


def backward(packed, upstream, fresh, segments):
    return pl.pallas_call(
        backward_kernel,
        out_shape=(
            jax.ShapeDtypeStruct(packed.shape, packed.dtype),
            jax.ShapeDtypeStruct((2, HEAD_SIZE), jnp.float32),
        ),
        grid=(1,),
        in_specs=[VMEM, VMEM, side_tile(fresh), VMEM],
        out_specs=(VMEM, VMEM),
        cost_estimate=cost(1024),
        compiler_params=pltpu.CompilerParams(vmem_limit_bytes=VMEM_LIMIT),
        name="backward",
    )(packed, upstream, fresh, segments)


def unpack_kernel(packed_ref, q_ref, kv_ref):
    q_width = q_ref.shape[1]
    q_ref[...] = packed_ref[:, :q_width]
    kv_ref[...] = packed_ref[:, q_width : q_width + kv_ref.shape[1]]


def unpack(packed, widths):
    return pl.pallas_call(
        unpack_kernel,
        out_shape=[
            jax.ShapeDtypeStruct((packed.shape[0], width), packed.dtype) for width in widths
        ],
        cost_estimate=cost(1024),
        compiler_params=pltpu.CompilerParams(vmem_limit_bytes=VMEM_LIMIT),
        name="unpack",
    )(packed)


def local(
    fresh_q, current_key_value, held_q, retained_key_value, cotangent, norm_gains, plan, segment_ids
):
    sections, replicas = lax.axis_size("section"), lax.axis_size("dp")
    opposite = [(i, -i % sections) for i in range(sections)]
    up = [(i, (i + 1) % sections) for i in range(sections)]
    down = [(i, (i - 1) % sections) for i in range(sections)]
    segments = segment_ids[0]
    widths = fresh_q.shape[2], current_key_value.shape[2]

    def hop(value, pairs):
        return lax.ppermute(value, "section", pairs)

    fresh = hop(pack(fresh_q[0], current_key_value[0], norm_gains[0], plan), up)
    held = hop(jnp.concatenate([held_q[0], retained_key_value[0]], axis=1), opposite)
    stored = hop(fresh, opposite)
    grad, gain = backward(held, cotangent[0], fresh, segments)
    grad = hop(grad, down)
    attention_out = forward(fresh, widths[0], segments)

    step = 1
    while 2 * step < replicas:
        gain = gain + lax.ppermute(gain, "dp", [(i, i ^ step) for i in range(replicas)])
        step *= 2
    halves = [
        lax.ppermute(
            gain,
            ("section", "dp"),
            [
                (i * replicas + j, (i - 1) % sections * replicas + (j ^ other))
                for i in range(sections)
                for j in range(replicas)
            ],
        )
        for other in (0, step)
    ]
    gain = (halves[0] + halves[1]) * (1.0 / replicas)
    stored_q, stored_kv = unpack(stored, widths)
    grad_q, grad_kv = unpack(grad, widths)
    return (
        attention_out[None],
        stored_q[None],
        stored_kv[None],
        grad_q[None],
        grad_kv[None],
        gain[None],
    )


def solution(mesh):
    rows = P("section", "dp", None)
    gains = P("section", None, None)
    return jax.shard_map(
        local,
        mesh=mesh,
        in_specs=(rows, rows, rows, rows, rows, gains, P("section", None), P("dp", None, None)),
        out_specs=(rows, rows, rows, rows, rows, gains),
        check_vma=False,
    )
```

```python
import functools
import math

import jax
import jax.numpy as jnp
from jax import lax
from jax.experimental import pallas as pl
from jax.experimental.pallas import tpu as pltpu
from jax.sharding import PartitionSpec as P

HEAD_SIZE = 128
EPSILON = 1e-06
SCORE_SCALE = 1.0 / math.sqrt(HEAD_SIZE)
EXP2_SCALE = SCORE_SCALE * math.log2(math.e)

VMEM_LIMIT = 16 << 20
CUT_NUM, CUT_DEN = 9, 20
NT = (((1,), (1,)), ((), ()))
TN = (((0,), (0,)), ((), ()))
NN = (((1,), (0,)), ((), ()))


def dot(a, b, dims):
    return lax.dot_general(a, b, dims, preferred_element_type=jnp.float32)


def head(ref, index):
    return ref[:, index * HEAD_SIZE : (index + 1) * HEAD_SIZE]


def stacked(ref, first, count):
    return jnp.concatenate([head(ref, first + i) for i in range(count)], axis=0)


def allowed_pairs(segment_ref, chosen, copies):
    micro, tokens = segment_ref.shape
    ids = segment_ref[...].astype(jnp.float32)
    number = lax.broadcasted_iota(jnp.int32, (micro, tokens), 0).astype(jnp.float32)
    row = jnp.sum(jnp.where(number == chosen[:, :tokens], ids, 0.0), axis=0, keepdims=True)
    keys_at = lax.broadcasted_iota(jnp.int32, (tokens, tokens), 0)
    queries_at = lax.broadcasted_iota(jnp.int32, (tokens, tokens), 1)
    column = jnp.sum(jnp.where(keys_at == queries_at, row, 0.0), axis=1, keepdims=True)
    allowed = ((keys_at <= queries_at) & (column == row)).astype(jnp.float32)
    return jnp.concatenate([allowed] * copies, axis=1) > 0.5


def normalized(values):
    wide = values.astype(jnp.float32)
    factor = lax.rsqrt(jnp.mean(wide * wide, axis=1, keepdims=True) + EPSILON)
    return wide * factor, factor


def probabilities(key, query, allowed):
    scores = dot(key, query, NT)
    weights = jnp.where(allowed, jnp.exp2(scores * EXP2_SCALE), 0.0)
    return weights * (1.0 / jnp.sum(weights, axis=0, keepdims=True))


def forward_kernel(packed_ref, side_ref, segment_ref, out_ref):
    side = side_ref[...]
    tokens = packed_ref.shape[0]
    heads = out_ref.shape[1] // HEAD_SIZE
    kv_heads = (packed_ref.shape[1] // HEAD_SIZE - heads) // 2
    per_kv = heads // kv_heads
    allowed = allowed_pairs(segment_ref, side[2:3], per_kv)
    for g in range(kv_heads):
        key_hat, _ = normalized(head(packed_ref, heads + g))
        key = (key_hat * side[1:2]).astype(jnp.bfloat16)
        value = head(packed_ref, heads + kv_heads + g)
        query_hat, _ = normalized(stacked(packed_ref, g * per_kv, per_kv))
        query = (query_hat * side[0:1]).astype(jnp.bfloat16)
        probs = probabilities(key, query, allowed).astype(jnp.bfloat16)
        out = dot(probs, value, TN).astype(jnp.bfloat16)
        for i in range(per_kv):
            h = g * per_kv + i
            out_ref[:, h * HEAD_SIZE : (h + 1) * HEAD_SIZE] = out[i * tokens : (i + 1) * tokens]


def norm_back(hat, factor, scaled_gain, d_normed):
    terms = d_normed * hat
    inner = jnp.sum(terms * scaled_gain, axis=1, keepdims=True) * (1.0 / HEAD_SIZE)
    return (d_normed * scaled_gain - hat * inner) * factor, terms


def summed_rows(terms):
    return jnp.sum(terms.reshape(-1, 8, terms.shape[1]), axis=0)


def backward_kernel(packed_ref, up_ref, side_ref, segment_ref, *outs):
    *grad_refs, gain_ref = outs

    def write(block, value):
        first = grad_refs[0].shape[1] // HEAD_SIZE
        ref, at = (grad_refs[0], block) if block < first else (grad_refs[1], block - first)
        ref[:, at * HEAD_SIZE : (at + 1) * HEAD_SIZE] = value.astype(jnp.bfloat16)

    side = side_ref[...]
    tokens = packed_ref.shape[0]
    heads = up_ref.shape[1] // HEAD_SIZE
    kv_heads = (packed_ref.shape[1] // HEAD_SIZE - heads) // 2
    per_kv = heads // kv_heads
    allowed = allowed_pairs(segment_ref, side[3:4], per_kv)
    q_gain, k_gain = side[0:1], side[1:2]
    q_terms = k_terms = 0.0
    for g in range(kv_heads):
        key_hat, key_factor = normalized(head(packed_ref, heads + g))
        key = (key_hat * k_gain).astype(jnp.bfloat16)
        value = head(packed_ref, heads + kv_heads + g)
        query_hat, query_factor = normalized(stacked(packed_ref, g * per_kv, per_kv))
        query = (query_hat * q_gain).astype(jnp.bfloat16)
        upstream = stacked(up_ref, g * per_kv, per_kv)
        probs = probabilities(key, query, allowed)
        d_probs = dot(value, upstream, NT)
        d_value = dot(probs.astype(jnp.bfloat16), upstream, NN)
        centre = jnp.sum(probs * d_probs, axis=0, keepdims=True)
        d_scores = (probs * (d_probs - centre)).astype(jnp.bfloat16)
        d_key = dot(d_scores, query, NN)
        d_query, terms = norm_back(
            query_hat, query_factor, q_gain * SCORE_SCALE, dot(d_scores, key, TN)
        )
        q_terms += summed_rows(terms)
        for i in range(per_kv):
            write(g * per_kv + i, d_query[i * tokens : (i + 1) * tokens])
        d_key, terms = norm_back(key_hat, key_factor, k_gain * SCORE_SCALE, d_key)
        k_terms += summed_rows(terms)
        write(heads + g, d_key)
        write(heads + kv_heads + g, d_value)
    gain_ref[0:1, :] = jnp.sum(q_terms, axis=0, keepdims=True) * SCORE_SCALE
    gain_ref[1:2, :] = jnp.sum(k_terms, axis=0, keepdims=True) * SCORE_SCALE


def cost(work):
    return pl.CostEstimate(flops=work, bytes_accessed=1024, transcendentals=0)


VMEM = pl.BlockSpec(memory_space=pltpu.VMEM)


def forward(fresh, q_width, side, segments):
    return pl.pallas_call(
        forward_kernel,
        out_shape=jax.ShapeDtypeStruct((fresh.shape[0], q_width), fresh.dtype),
        in_specs=[VMEM] * 3,
        out_specs=VMEM,
        cost_estimate=cost(1024),
        compiler_params=pltpu.CompilerParams(vmem_limit_bytes=VMEM_LIMIT),
        name="forward",
    )(fresh, side, segments)


def backward(packed, upstream, side, segments):
    tokens, width = packed.shape
    cut = width // HEAD_SIZE * CUT_NUM // CUT_DEN * HEAD_SIZE
    return pl.pallas_call(
        backward_kernel,
        out_shape=[jax.ShapeDtypeStruct((tokens, w), packed.dtype) for w in (cut, width - cut)]
        + [jax.ShapeDtypeStruct((2, HEAD_SIZE), jnp.float32)],
        in_specs=[VMEM] * 4,
        out_specs=[VMEM] * 3,
        cost_estimate=cost(1024),
        compiler_params=pltpu.CompilerParams(vmem_limit_bytes=VMEM_LIMIT),
        name="backward",
    )(packed, upstream, side, segments)


def unpack_kernel(packed_ref, q_ref, kv_ref):
    q_width = q_ref.shape[1]
    q_ref[...] = packed_ref[:, :q_width]
    kv_ref[...] = packed_ref[:, q_width : q_width + kv_ref.shape[1]]


def unpack(packed, widths):
    return pl.pallas_call(
        unpack_kernel,
        out_shape=[
            jax.ShapeDtypeStruct((packed.shape[0], width), packed.dtype) for width in widths
        ],
        cost_estimate=cost(1024),
        compiler_params=pltpu.CompilerParams(vmem_limit_bytes=VMEM_LIMIT),
        name="unpack",
    )(packed)


def merge_kernel(first_ref, second_ref, q_ref, kv_ref):
    cut, q_width = first_ref.shape[1], q_ref.shape[1]
    q_ref[:, :cut] = first_ref[...]
    q_ref[:, cut:] = second_ref[:, : q_width - cut]
    kv_ref[...] = second_ref[:, q_width - cut :]


def merge(grads, widths):
    return pl.pallas_call(
        merge_kernel,
        out_shape=[
            jax.ShapeDtypeStruct((grads[0].shape[0], width), grads[0].dtype) for width in widths
        ],
        cost_estimate=cost(1024),
        compiler_params=pltpu.CompilerParams(vmem_limit_bytes=VMEM_LIMIT),
        name="merge",
    )(*grads)


def local(
    fresh_q, current_key_value, held_q, retained_key_value, cotangent, norm_gains, plan, segment_ids
):
    sections, replicas = lax.axis_size("section"), lax.axis_size("dp")
    opposite = [(i, -i % sections) for i in range(sections)]
    up = [(i, (i + 1) % sections) for i in range(sections)]
    down = [(i, (i - 1) % sections) for i in range(sections)]
    segments = segment_ids[0]
    widths = fresh_q.shape[2], current_key_value.shape[2]

    def hop(value, pairs):
        return lax.ppermute(value, "section", pairs)

    numbers = jnp.broadcast_to(plan[0].astype(jnp.float32)[:, None], (2, HEAD_SIZE))
    fresh = hop(jnp.concatenate([fresh_q[0], current_key_value[0]], axis=1), up)
    held = hop(jnp.concatenate([held_q[0], retained_key_value[0]], axis=1), opposite)
    side = hop(jnp.concatenate([norm_gains[0], numbers], axis=0), up)
    stored = hop(fresh, opposite)
    first, second, gain = backward(held, cotangent[0], side, segments)
    fixed = [i for i in range(sections) if -i % sections == i]
    across = [(i, (i + sections // 2) % sections) for i in fixed]
    after = [(j, (i - 1) % sections) for i, j in across]
    straight = [(i, (i - 1) % sections) for i in range(sections) if i not in fixed]
    crossed = hop(first, across)
    me = lax.axis_index("section")
    stays = functools.reduce(jnp.logical_or, [me == i for i in fixed])
    first = hop(jnp.where(stays, crossed, first), after + straight)
    second = hop(second, down)
    attention_out = forward(fresh, widths[0], side, segments)

    step = 1
    while 2 * step < replicas:
        gain = gain + lax.ppermute(gain, "dp", [(i, i ^ step) for i in range(replicas)])
        step *= 2
    halves = [
        lax.ppermute(
            gain,
            ("section", "dp"),
            [
                (i * replicas + j, (i - 1) % sections * replicas + (j ^ other))
                for i in range(sections)
                for j in range(replicas)
            ],
        )
        for other in (0, step)
    ]
    stored_q, stored_kv = unpack(stored, widths)
    grad_q, grad_kv = merge((first, second), widths)
    *halves, grad_q, stored_q = lax.optimization_barrier((*halves, grad_q, stored_q))
    gain = (halves[0] + halves[1]) * (1.0 / replicas)
    return (
        attention_out[None],
        stored_q[None],
        stored_kv[None],
        grad_q[None],
        grad_kv[None],
        gain[None],
    )


def solution(mesh):
    rows = P("section", "dp", None)
    gains = P("section", None, None)
    return jax.shard_map(
        local,
        mesh=mesh,
        in_specs=(rows, rows, rows, rows, rows, gains, P("section", None), P("dp", None, None)),
        out_specs=(rows, rows, rows, rows, rows, gains),
        check_vma=False,
    )
```

```python
import functools
import math

import jax
import jax.numpy as jnp
from jax import lax
from jax.experimental import pallas as pl
from jax.experimental.pallas import tpu as pltpu
from jax.sharding import PartitionSpec as P

HEAD_SIZE = 128
EPSILON = 1e-06
SCORE_SCALE = 1.0 / math.sqrt(HEAD_SIZE)
EXP2_SCALE = SCORE_SCALE * math.log2(math.e)

VMEM_LIMIT = 16 << 20
CUT_NUM, CUT_DEN = 10, 20
NT = (((1,), (1,)), ((), ()))
TN = (((0,), (0,)), ((), ()))
NN = (((1,), (0,)), ((), ()))


def dot(a, b, dims):
    return lax.dot_general(a, b, dims, preferred_element_type=jnp.float32)


def head(ref, index):
    return ref[:, index * HEAD_SIZE : (index + 1) * HEAD_SIZE]


def stacked(ref, first, count):
    return jnp.concatenate([head(ref, first + i) for i in range(count)], axis=0)


def allowed_pairs(segment_ref, chosen, copies):
    micro, tokens = segment_ref.shape
    ids = segment_ref[...].astype(jnp.float32)
    number = lax.broadcasted_iota(jnp.int32, (micro, tokens), 0).astype(jnp.float32)
    row = jnp.sum(jnp.where(number == chosen[:, :tokens], ids, 0.0), axis=0, keepdims=True)
    keys_at = lax.broadcasted_iota(jnp.int32, (tokens, tokens), 0)
    queries_at = lax.broadcasted_iota(jnp.int32, (tokens, tokens), 1)
    column = jnp.sum(jnp.where(keys_at == queries_at, row, 0.0), axis=1, keepdims=True)
    allowed = ((keys_at <= queries_at) & (column == row)).astype(jnp.float32)
    return jnp.concatenate([allowed] * copies, axis=1) > 0.5


def normalized(values):
    wide = values.astype(jnp.float32)
    factor = lax.rsqrt(jnp.mean(wide * wide, axis=1, keepdims=True) + EPSILON)
    return wide * factor, factor


def probabilities(key, query, allowed):
    scores = dot(key, query, NT)
    weights = jnp.where(allowed, jnp.exp2(scores * EXP2_SCALE), 0.0)
    return weights * (1.0 / jnp.sum(weights, axis=0, keepdims=True))


def forward_kernel(packed_ref, side_ref, segment_ref, out_ref):
    side = side_ref[...]
    tokens = packed_ref.shape[0]
    heads = out_ref.shape[1] // HEAD_SIZE
    kv_heads = (packed_ref.shape[1] // HEAD_SIZE - heads) // 2
    per_kv = heads // kv_heads
    allowed = allowed_pairs(segment_ref, side[2:3], per_kv)
    for g in range(kv_heads):
        key_hat, _ = normalized(head(packed_ref, heads + g))
        key = (key_hat * side[1:2]).astype(jnp.bfloat16)
        value = head(packed_ref, heads + kv_heads + g)
        query_hat, _ = normalized(stacked(packed_ref, g * per_kv, per_kv))
        query = (query_hat * side[0:1]).astype(jnp.bfloat16)
        probs = probabilities(key, query, allowed).astype(jnp.bfloat16)
        out = dot(probs, value, TN).astype(jnp.bfloat16)
        for i in range(per_kv):
            h = g * per_kv + i
            out_ref[:, h * HEAD_SIZE : (h + 1) * HEAD_SIZE] = out[i * tokens : (i + 1) * tokens]


def norm_back(hat, factor, scaled_gain, d_normed):
    terms = d_normed * hat
    inner = jnp.sum(terms * scaled_gain, axis=1, keepdims=True) * (1.0 / HEAD_SIZE)
    return (d_normed * scaled_gain - hat * inner) * factor, terms


def summed_rows(terms):
    return jnp.sum(terms.reshape(-1, 8, terms.shape[1]), axis=0)


def backward_kernel(packed_ref, up_ref, side_ref, segment_ref, *outs):
    *grad_refs, gain_ref = outs

    def write(block, value):
        first = grad_refs[0].shape[1] // HEAD_SIZE
        ref, at = (grad_refs[0], block) if block < first else (grad_refs[1], block - first)
        ref[:, at * HEAD_SIZE : (at + 1) * HEAD_SIZE] = value.astype(jnp.bfloat16)

    side = side_ref[...]
    tokens = packed_ref.shape[0]
    heads = up_ref.shape[1] // HEAD_SIZE
    kv_heads = (packed_ref.shape[1] // HEAD_SIZE - heads) // 2
    per_kv = heads // kv_heads
    allowed = allowed_pairs(segment_ref, side[3:4], per_kv)
    q_gain, k_gain = side[0:1], side[1:2]
    q_terms = k_terms = 0.0
    for g in range(kv_heads):
        key_hat, key_factor = normalized(head(packed_ref, heads + g))
        key = (key_hat * k_gain).astype(jnp.bfloat16)
        value = head(packed_ref, heads + kv_heads + g)
        query_hat, query_factor = normalized(stacked(packed_ref, g * per_kv, per_kv))
        query = (query_hat * q_gain).astype(jnp.bfloat16)
        upstream = stacked(up_ref, g * per_kv, per_kv)
        probs = probabilities(key, query, allowed)
        d_probs = dot(value, upstream, NT)
        d_value = dot(probs.astype(jnp.bfloat16), upstream, NN)
        centre = jnp.sum(probs * d_probs, axis=0, keepdims=True)
        d_scores = (probs * (d_probs - centre)).astype(jnp.bfloat16)
        d_key = dot(d_scores, query, NN)
        d_query, terms = norm_back(
            query_hat, query_factor, q_gain * SCORE_SCALE, dot(d_scores, key, TN)
        )
        q_terms += summed_rows(terms)
        for i in range(per_kv):
            write(g * per_kv + i, d_query[i * tokens : (i + 1) * tokens])
        d_key, terms = norm_back(key_hat, key_factor, k_gain * SCORE_SCALE, d_key)
        k_terms += summed_rows(terms)
        write(heads + g, d_key)
        write(heads + kv_heads + g, d_value)
    gain_ref[0:1, :] = jnp.sum(q_terms, axis=0, keepdims=True) * SCORE_SCALE
    gain_ref[1:2, :] = jnp.sum(k_terms, axis=0, keepdims=True) * SCORE_SCALE


def cost(work):
    return pl.CostEstimate(flops=work, bytes_accessed=1024, transcendentals=0)


VMEM = pl.BlockSpec(memory_space=pltpu.VMEM)


def forward(fresh, q_width, side, segments):
    return pl.pallas_call(
        forward_kernel,
        out_shape=jax.ShapeDtypeStruct((fresh.shape[0], q_width), fresh.dtype),
        in_specs=[VMEM] * 3,
        out_specs=VMEM,
        cost_estimate=cost(1024),
        compiler_params=pltpu.CompilerParams(vmem_limit_bytes=VMEM_LIMIT),
        name="forward",
    )(fresh, side, segments)


def backward(packed, upstream, side, segments):
    tokens, width = packed.shape
    cut = width // HEAD_SIZE * CUT_NUM // CUT_DEN * HEAD_SIZE
    return pl.pallas_call(
        backward_kernel,
        out_shape=[jax.ShapeDtypeStruct((tokens, w), packed.dtype) for w in (cut, width - cut)]
        + [jax.ShapeDtypeStruct((2, HEAD_SIZE), jnp.float32)],
        in_specs=[VMEM] * 4,
        out_specs=[VMEM] * 3,
        cost_estimate=cost(1024),
        compiler_params=pltpu.CompilerParams(vmem_limit_bytes=VMEM_LIMIT),
        name="backward",
    )(packed, upstream, side, segments)


def unpack_kernel(packed_ref, q_ref, kv_ref):
    q_width = q_ref.shape[1]
    q_ref[...] = packed_ref[:, :q_width]
    kv_ref[...] = packed_ref[:, q_width : q_width + kv_ref.shape[1]]


def unpack(packed, widths):
    return pl.pallas_call(
        unpack_kernel,
        out_shape=[
            jax.ShapeDtypeStruct((packed.shape[0], width), packed.dtype) for width in widths
        ],
        cost_estimate=cost(1024),
        compiler_params=pltpu.CompilerParams(vmem_limit_bytes=VMEM_LIMIT),
        name="unpack",
    )(packed)


def merge_kernel(first_ref, second_ref, q_ref, kv_ref):
    cut, q_width = first_ref.shape[1], q_ref.shape[1]
    q_ref[:, :cut] = first_ref[...]
    q_ref[:, cut:] = second_ref[:, : q_width - cut]
    kv_ref[...] = second_ref[:, q_width - cut :]


def merge(grads, widths):
    return pl.pallas_call(
        merge_kernel,
        out_shape=[
            jax.ShapeDtypeStruct((grads[0].shape[0], width), grads[0].dtype) for width in widths
        ],
        cost_estimate=cost(1024),
        compiler_params=pltpu.CompilerParams(vmem_limit_bytes=VMEM_LIMIT),
        name="merge",
    )(*grads)


def local(
    fresh_q, current_key_value, held_q, retained_key_value, cotangent, norm_gains, plan, segment_ids
):
    sections, replicas = lax.axis_size("section"), lax.axis_size("dp")
    opposite = [(i, -i % sections) for i in range(sections)]
    up = [(i, (i + 1) % sections) for i in range(sections)]
    down = [(i, (i - 1) % sections) for i in range(sections)]
    segments = segment_ids[0]
    widths = fresh_q.shape[2], current_key_value.shape[2]

    def hop(value, pairs):
        return lax.ppermute(value, "section", pairs)

    numbers = jnp.broadcast_to(plan[0].astype(jnp.float32)[:, None], (2, HEAD_SIZE))
    fresh = hop(jnp.concatenate([fresh_q[0], current_key_value[0]], axis=1), up)
    held = hop(jnp.concatenate([held_q[0], retained_key_value[0]], axis=1), opposite)
    side = hop(jnp.concatenate([norm_gains[0], numbers], axis=0), up)
    stored = hop(fresh, opposite)
    first, second, gain = backward(held, cotangent[0], side, segments)
    fixed = [i for i in range(sections) if -i % sections == i]
    across = [(i, (i + sections // 2) % sections) for i in fixed]
    after = [(j, (i - 1) % sections) for i, j in across]
    straight = [(i, (i - 1) % sections) for i in range(sections) if i not in fixed]
    crossed = hop(first, across)
    me = lax.axis_index("section")
    stays = functools.reduce(jnp.logical_or, [me == i for i in fixed])
    second = hop(second, down)
    step = 1
    while 2 * step < replicas:
        gain = gain + lax.ppermute(gain, "dp", [(i, i ^ step) for i in range(replicas)])
        step *= 2
    crossed, second, gain = lax.optimization_barrier((crossed, second, gain))
    first = jnp.where(stays, crossed, first)
    first = hop(first, after + straight)
    attention_out = forward(fresh, widths[0], side, segments)

    halves = [
        lax.ppermute(
            gain,
            ("section", "dp"),
            [
                (i * replicas + j, (i - 1) % sections * replicas + (j ^ other))
                for i in range(sections)
                for j in range(replicas)
            ],
        )
        for other in (0, step)
    ]
    stored_q, stored_kv = unpack(stored, widths)
    grad_q, grad_kv = merge((first, second), widths)
    *halves, grad_q = lax.optimization_barrier((*halves, grad_q))
    gain = (halves[0] + halves[1]) * (1.0 / replicas)
    return (
        attention_out[None],
        stored_q[None],
        stored_kv[None],
        grad_q[None],
        grad_kv[None],
        gain[None],
    )


def solution(mesh):
    rows = P("section", "dp", None)
    gains = P("section", None, None)
    return jax.shard_map(
        local,
        mesh=mesh,
        in_specs=(rows, rows, rows, rows, rows, gains, P("section", None), P("dp", None, None)),
        out_specs=(rows, rows, rows, rows, rows, gains),
        check_vma=False,
    )
```

```python
import functools
import math

import jax
import jax.numpy as jnp
from jax import lax
from jax.experimental import pallas as pl
from jax.experimental.pallas import tpu as pltpu
from jax.sharding import PartitionSpec as P

HEAD_SIZE = 128
EPSILON = 1e-06
SCORE_SCALE = 1.0 / math.sqrt(HEAD_SIZE)
EXP2_SCALE = SCORE_SCALE * math.log2(math.e)

VMEM_LIMIT = 16 << 20
CUT_NUM, CUT_DEN = 10, 20
NT = (((1,), (1,)), ((), ()))
TN = (((0,), (0,)), ((), ()))
NN = (((1,), (0,)), ((), ()))


def dot(a, b, dims):
    return lax.dot_general(a, b, dims, preferred_element_type=jnp.float32)


def head(ref, index):
    return ref[:, index * HEAD_SIZE : (index + 1) * HEAD_SIZE]


def stacked(ref, first, count):
    return jnp.concatenate([head(ref, first + i) for i in range(count)], axis=0)


def allowed_pairs(segment_ref, chosen, copies):
    micro, tokens = segment_ref.shape
    ids = segment_ref[...].astype(jnp.float32)
    number = lax.broadcasted_iota(jnp.int32, (micro, tokens), 0).astype(jnp.float32)
    row = jnp.sum(jnp.where(number == chosen[:, :tokens], ids, 0.0), axis=0, keepdims=True)
    keys_at = lax.broadcasted_iota(jnp.int32, (tokens, tokens), 0)
    queries_at = lax.broadcasted_iota(jnp.int32, (tokens, tokens), 1)
    column = jnp.sum(jnp.where(keys_at == queries_at, row, 0.0), axis=1, keepdims=True)
    allowed = ((keys_at <= queries_at) & (column == row)).astype(jnp.float32)
    return jnp.concatenate([allowed] * copies, axis=1) > 0.5


def normalized(values):
    wide = values.astype(jnp.float32)
    factor = lax.rsqrt(jnp.mean(wide * wide, axis=1, keepdims=True) + EPSILON)
    return wide * factor, factor


def probabilities(key, query, allowed):
    scores = dot(key, query, NT)
    weights = jnp.where(allowed, jnp.exp2(scores * EXP2_SCALE), 0.0)
    return weights * (1.0 / jnp.sum(weights, axis=0, keepdims=True))


def forward_kernel(packed_ref, side_ref, segment_ref, out_ref):
    side = side_ref[...]
    tokens = packed_ref.shape[0]
    heads = out_ref.shape[1] // HEAD_SIZE
    kv_heads = (packed_ref.shape[1] // HEAD_SIZE - heads) // 2
    per_kv = heads // kv_heads
    allowed = allowed_pairs(segment_ref, side[2:3], per_kv)
    for g in range(kv_heads):
        key_hat, _ = normalized(head(packed_ref, heads + g))
        key = (key_hat * side[1:2]).astype(jnp.bfloat16)
        value = head(packed_ref, heads + kv_heads + g)
        query_hat, _ = normalized(stacked(packed_ref, g * per_kv, per_kv))
        query = (query_hat * side[0:1]).astype(jnp.bfloat16)
        probs = probabilities(key, query, allowed).astype(jnp.bfloat16)
        out = dot(probs, value, TN).astype(jnp.bfloat16)
        for i in range(per_kv):
            h = g * per_kv + i
            out_ref[:, h * HEAD_SIZE : (h + 1) * HEAD_SIZE] = out[i * tokens : (i + 1) * tokens]


def norm_back(hat, factor, scaled_gain, d_normed):
    terms = d_normed * hat
    inner = jnp.sum(terms * scaled_gain, axis=1, keepdims=True) * (1.0 / HEAD_SIZE)
    return (d_normed * scaled_gain - hat * inner) * factor, terms


def summed_rows(terms):
    return jnp.sum(terms.reshape(-1, 8, terms.shape[1]), axis=0)


def backward_kernel(packed_ref, up_ref, side_ref, segment_ref, *outs):
    *grad_refs, gain_ref = outs

    def write(block, value):
        first = grad_refs[0].shape[1] // HEAD_SIZE
        ref, at = (grad_refs[0], block) if block < first else (grad_refs[1], block - first)
        ref[:, at * HEAD_SIZE : (at + 1) * HEAD_SIZE] = value.astype(jnp.bfloat16)

    side = side_ref[...]
    tokens = packed_ref.shape[0]
    heads = up_ref.shape[1] // HEAD_SIZE
    kv_heads = (packed_ref.shape[1] // HEAD_SIZE - heads) // 2
    per_kv = heads // kv_heads
    allowed = allowed_pairs(segment_ref, side[3:4], per_kv)
    q_gain, k_gain = side[0:1], side[1:2]
    q_terms = k_terms = 0.0
    for g in range(kv_heads):
        key_hat, key_factor = normalized(head(packed_ref, heads + g))
        key = (key_hat * k_gain).astype(jnp.bfloat16)
        value = head(packed_ref, heads + kv_heads + g)
        query_hat, query_factor = normalized(stacked(packed_ref, g * per_kv, per_kv))
        query = (query_hat * q_gain).astype(jnp.bfloat16)
        upstream = stacked(up_ref, g * per_kv, per_kv)
        probs = probabilities(key, query, allowed)
        d_probs = dot(value, upstream, NT)
        d_value = dot(probs.astype(jnp.bfloat16), upstream, NN)
        centre = jnp.sum(probs * d_probs, axis=0, keepdims=True)
        d_scores = (probs * (d_probs - centre)).astype(jnp.bfloat16)
        d_key = dot(d_scores, query, NN)
        d_query, terms = norm_back(
            query_hat, query_factor, q_gain * SCORE_SCALE, dot(d_scores, key, TN)
        )
        q_terms += summed_rows(terms)
        for i in range(per_kv):
            write(g * per_kv + i, d_query[i * tokens : (i + 1) * tokens])
        d_key, terms = norm_back(key_hat, key_factor, k_gain * SCORE_SCALE, d_key)
        k_terms += summed_rows(terms)
        write(heads + g, d_key)
        write(heads + kv_heads + g, d_value)
    gain_ref[0:1, :] = jnp.sum(q_terms, axis=0, keepdims=True) * SCORE_SCALE
    gain_ref[1:2, :] = jnp.sum(k_terms, axis=0, keepdims=True) * SCORE_SCALE


def cost(work):
    return pl.CostEstimate(flops=work, bytes_accessed=1024, transcendentals=0)


VMEM = pl.BlockSpec(memory_space=pltpu.VMEM)


def forward(fresh, q_width, side, segments):
    return pl.pallas_call(
        forward_kernel,
        out_shape=jax.ShapeDtypeStruct((fresh.shape[0], q_width), fresh.dtype),
        in_specs=[VMEM] * 3,
        out_specs=VMEM,
        cost_estimate=cost(1024),
        compiler_params=pltpu.CompilerParams(vmem_limit_bytes=VMEM_LIMIT),
        name="forward",
    )(fresh, side, segments)


def backward(packed, upstream, side, segments):
    tokens, width = packed.shape
    cut = width // HEAD_SIZE * CUT_NUM // CUT_DEN * HEAD_SIZE
    return pl.pallas_call(
        backward_kernel,
        out_shape=[jax.ShapeDtypeStruct((tokens, w), packed.dtype) for w in (cut, width - cut)]
        + [jax.ShapeDtypeStruct((2, HEAD_SIZE), jnp.float32)],
        in_specs=[VMEM] * 4,
        out_specs=[VMEM] * 3,
        cost_estimate=cost(1024),
        compiler_params=pltpu.CompilerParams(vmem_limit_bytes=VMEM_LIMIT),
        name="backward",
    )(packed, upstream, side, segments)


def unpack_kernel(share, packed_ref, here_ref, there_ref, q_ref, kv_ref, gain_ref):
    q_width = q_ref.shape[1]
    q_ref[...] = packed_ref[:, :q_width]
    kv_ref[...] = packed_ref[:, q_width : q_width + kv_ref.shape[1]]
    gain_ref[...] = (here_ref[...] + there_ref[...]) * share


def unpack(packed, halves, widths, share):
    shapes = [jax.ShapeDtypeStruct((packed.shape[0], width), packed.dtype) for width in widths]
    return pl.pallas_call(
        functools.partial(unpack_kernel, share),
        out_shape=shapes + [jax.ShapeDtypeStruct(halves[0].shape, halves[0].dtype)],
        cost_estimate=cost(1024),
        compiler_params=pltpu.CompilerParams(vmem_limit_bytes=VMEM_LIMIT),
        name="unpack",
    )(packed, *halves)


def merge_kernel(first_ref, second_ref, q_ref, kv_ref):
    cut, q_width = first_ref.shape[1], q_ref.shape[1]
    q_ref[:, :cut] = first_ref[...]
    q_ref[:, cut:] = second_ref[:, : q_width - cut]
    kv_ref[...] = second_ref[:, q_width - cut :]


def merge(grads, widths):
    return pl.pallas_call(
        merge_kernel,
        out_shape=[
            jax.ShapeDtypeStruct((grads[0].shape[0], width), grads[0].dtype) for width in widths
        ],
        cost_estimate=cost(1024),
        compiler_params=pltpu.CompilerParams(vmem_limit_bytes=VMEM_LIMIT),
        name="merge",
    )(*grads)


def local(
    fresh_q, current_key_value, held_q, retained_key_value, cotangent, norm_gains, plan, segment_ids
):
    sections, replicas = lax.axis_size("section"), lax.axis_size("dp")
    opposite = [(i, -i % sections) for i in range(sections)]
    up = [(i, (i + 1) % sections) for i in range(sections)]
    down = [(i, (i - 1) % sections) for i in range(sections)]
    segments = segment_ids[0]
    widths = fresh_q.shape[2], current_key_value.shape[2]

    def hop(value, pairs):
        return lax.ppermute(value, "section", pairs)

    numbers = jnp.broadcast_to(plan[0].astype(jnp.float32)[:, None], (2, HEAD_SIZE))
    fresh = hop(jnp.concatenate([fresh_q[0], current_key_value[0]], axis=1), up)
    held = hop(jnp.concatenate([held_q[0], retained_key_value[0]], axis=1), opposite)
    side = hop(jnp.concatenate([norm_gains[0], numbers], axis=0), up)
    stored = hop(fresh, opposite)
    first, second, gain = backward(held, cotangent[0], side, segments)
    fixed = [i for i in range(sections) if -i % sections == i]
    across = [(i, (i + sections // 2) % sections) for i in fixed]
    after = [(j, (i - 1) % sections) for i, j in across]
    straight = [(i, (i - 1) % sections) for i in range(sections) if i not in fixed]
    crossed = hop(first, across)
    me = lax.axis_index("section")
    stays = functools.reduce(jnp.logical_or, [me == i for i in fixed])
    second = hop(second, down)
    step = 1
    while 2 * step < replicas:
        gain = gain + lax.ppermute(gain, "dp", [(i, i ^ step) for i in range(replicas)])
        step *= 2
    crossed, second, gain = lax.optimization_barrier((crossed, second, gain))
    first = jnp.where(stays, crossed, first)
    first = hop(first, after + straight)
    attention_out = forward(fresh, widths[0], side, segments)

    halves = [
        lax.ppermute(
            gain,
            ("section", "dp"),
            [
                (i * replicas + j, (i - 1) % sections * replicas + (j ^ other))
                for i in range(sections)
                for j in range(replicas)
            ],
        )
        for other in (0, step)
    ]
    grad_q, grad_kv = merge((first, second), widths)
    stored, grad_q = lax.optimization_barrier((stored, grad_q))
    stored_q, stored_kv, gain = unpack(stored, halves, widths, 1.0 / replicas)
    return (
        attention_out[None],
        stored_q[None],
        stored_kv[None],
        grad_q[None],
        grad_kv[None],
        gain[None],
    )


def solution(mesh):
    rows = P("section", "dp", None)
    gains = P("section", None, None)
    return jax.shard_map(
        local,
        mesh=mesh,
        in_specs=(rows, rows, rows, rows, rows, gains, P("section", None), P("dp", None, None)),
        out_specs=(rows, rows, rows, rows, rows, gains),
        check_vma=False,
    )
```

```python
import functools
import math

import jax
import jax.numpy as jnp
from jax import lax
from jax.experimental import pallas as pl
from jax.experimental.pallas import tpu as pltpu
from jax.sharding import PartitionSpec as P

HEAD_SIZE = 128
EPSILON = 1e-06
SCORE_SCALE = 1.0 / math.sqrt(HEAD_SIZE)
EXP2_SCALE = SCORE_SCALE * math.log2(math.e)

VMEM_LIMIT = 16 << 20
NT = (((1,), (1,)), ((), ()))
TN = (((0,), (0,)), ((), ()))
NN = (((1,), (0,)), ((), ()))


def dot(a, b, dims):
    return lax.dot_general(a, b, dims, preferred_element_type=jnp.float32)


def head(ref, index):
    return ref[:, index * HEAD_SIZE : (index + 1) * HEAD_SIZE]


def stacked(ref, first, count):
    return jnp.concatenate([head(ref, first + i) for i in range(count)], axis=0)


def allowed_pairs(segment_ref, chosen, copies):
    micro, tokens = segment_ref.shape
    ids = segment_ref[...].astype(jnp.float32)
    number = lax.broadcasted_iota(jnp.int32, (micro, tokens), 0).astype(jnp.float32)
    row = jnp.sum(jnp.where(number == chosen[:, :tokens], ids, 0.0), axis=0, keepdims=True)
    keys_at = lax.broadcasted_iota(jnp.int32, (tokens, tokens), 0)
    queries_at = lax.broadcasted_iota(jnp.int32, (tokens, tokens), 1)
    column = jnp.sum(jnp.where(keys_at == queries_at, row, 0.0), axis=1, keepdims=True)
    allowed = ((keys_at <= queries_at) & (column == row)).astype(jnp.float32)
    return jnp.concatenate([allowed] * copies, axis=1) > 0.5


def normalized(values):
    wide = values.astype(jnp.float32)
    factor = lax.rsqrt(jnp.mean(wide * wide, axis=1, keepdims=True) + EPSILON)
    return wide * factor, factor


def probabilities(key, query, allowed):
    scores = dot(key, query, NT)
    weights = jnp.where(allowed, jnp.exp2(scores * EXP2_SCALE), 0.0)
    return weights * (1.0 / jnp.sum(weights, axis=0, keepdims=True))


def forward_kernel(packed_ref, side_ref, segment_ref, out_ref):
    side = side_ref[...]
    tokens = packed_ref.shape[0]
    heads = out_ref.shape[1] // HEAD_SIZE
    kv_heads = (packed_ref.shape[1] // HEAD_SIZE - heads) // 2
    per_kv = heads // kv_heads
    allowed = allowed_pairs(segment_ref, side[2:3], per_kv)
    for g in range(kv_heads):
        key_hat, _ = normalized(head(packed_ref, heads + g))
        key = (key_hat * side[1:2]).astype(jnp.bfloat16)
        value = head(packed_ref, heads + kv_heads + g)
        query_hat, _ = normalized(stacked(packed_ref, g * per_kv, per_kv))
        query = (query_hat * side[0:1]).astype(jnp.bfloat16)
        probs = probabilities(key, query, allowed).astype(jnp.bfloat16)
        out = dot(probs, value, TN).astype(jnp.bfloat16)
        for i in range(per_kv):
            h = g * per_kv + i
            out_ref[:, h * HEAD_SIZE : (h + 1) * HEAD_SIZE] = out[i * tokens : (i + 1) * tokens]


def norm_back(hat, factor, scaled_gain, d_normed):
    terms = d_normed * hat
    inner = jnp.sum(terms * scaled_gain, axis=1, keepdims=True) * (1.0 / HEAD_SIZE)
    return (d_normed * scaled_gain - hat * inner) * factor, terms


def summed_rows(terms):
    return jnp.sum(terms.reshape(-1, 8, terms.shape[1]), axis=0)


def backward_kernel(g, kv_heads, packed_ref, up_ref, side_ref, segment_ref, grad_ref, gain_ref):
    tokens = packed_ref.shape[0]
    heads = up_ref.shape[1] // HEAD_SIZE
    per_kv = heads // kv_heads
    allowed = allowed_pairs(segment_ref, side_ref[3:4, :], per_kv)
    q_gain, k_gain = side_ref[0:1, :], side_ref[1:2, :]
    key_hat, key_factor = normalized(head(packed_ref, heads + g))
    key = (key_hat * k_gain).astype(jnp.bfloat16)
    value = head(packed_ref, heads + kv_heads + g)
    query_hat, query_factor = normalized(stacked(packed_ref, g * per_kv, per_kv))
    query = (query_hat * q_gain).astype(jnp.bfloat16)
    upstream = stacked(up_ref, g * per_kv, per_kv)
    probs = probabilities(key, query, allowed)
    d_probs = dot(value, upstream, NT)
    d_value = dot(probs.astype(jnp.bfloat16), upstream, NN)
    centre = jnp.sum(probs * d_probs, axis=0, keepdims=True)
    d_scores = (probs * (d_probs - centre)).astype(jnp.bfloat16)
    d_key = dot(d_scores, query, NN)
    d_query, terms = norm_back(query_hat, query_factor, q_gain * SCORE_SCALE, dot(d_scores, key, TN))
    gain_ref[0:1, :] = jnp.sum(summed_rows(terms), axis=0, keepdims=True) * SCORE_SCALE
    d_query = d_query.astype(jnp.bfloat16)
    for i in range(per_kv):
        grad_ref[:, i * HEAD_SIZE : (i + 1) * HEAD_SIZE] = d_query[i * tokens : (i + 1) * tokens]
    d_key, terms = norm_back(key_hat, key_factor, k_gain * SCORE_SCALE, d_key)
    gain_ref[1:2, :] = jnp.sum(summed_rows(terms), axis=0, keepdims=True) * SCORE_SCALE
    at = per_kv * HEAD_SIZE
    grad_ref[:, at : at + HEAD_SIZE] = d_key.astype(jnp.bfloat16)
    grad_ref[:, at + HEAD_SIZE :] = d_value.astype(jnp.bfloat16)


def cost(work):
    return pl.CostEstimate(flops=work, bytes_accessed=1024, transcendentals=0)


VMEM = pl.BlockSpec(memory_space=pltpu.VMEM)


def forward(fresh, q_width, side, segments):
    return pl.pallas_call(
        forward_kernel,
        out_shape=jax.ShapeDtypeStruct((fresh.shape[0], q_width), fresh.dtype),
        in_specs=[VMEM] * 3,
        out_specs=VMEM,
        cost_estimate=cost(1024),
        compiler_params=pltpu.CompilerParams(vmem_limit_bytes=VMEM_LIMIT),
        name="forward",
    )(fresh, side, segments)


def backward(g, kv_heads, packed, upstream, side, segments):
    tokens, width = packed.shape
    return pl.pallas_call(
        functools.partial(backward_kernel, g, kv_heads),
        out_shape=[
            jax.ShapeDtypeStruct((tokens, width // kv_heads), packed.dtype),
            jax.ShapeDtypeStruct((2, HEAD_SIZE), jnp.float32),
        ],
        in_specs=[VMEM] * 4,
        out_specs=[VMEM] * 2,
        cost_estimate=cost(1024),
        compiler_params=pltpu.CompilerParams(vmem_limit_bytes=VMEM_LIMIT),
        name="backward",
    )(packed, upstream, side, segments)


def unpack_kernel(share, packed_ref, here_ref, there_ref, q_ref, kv_ref, gain_ref):
    q_width = q_ref.shape[1]
    q_ref[...] = packed_ref[:, :q_width]
    kv_ref[...] = packed_ref[:, q_width : q_width + kv_ref.shape[1]]
    gain_ref[...] = (here_ref[...] + there_ref[...]) * share


def unpack(packed, halves, widths, share):
    shapes = [jax.ShapeDtypeStruct((packed.shape[0], width), packed.dtype) for width in widths]
    return pl.pallas_call(
        functools.partial(unpack_kernel, share),
        out_shape=shapes + [jax.ShapeDtypeStruct(halves[0].shape, halves[0].dtype)],
        cost_estimate=cost(1024),
        compiler_params=pltpu.CompilerParams(vmem_limit_bytes=VMEM_LIMIT),
        name="unpack",
    )(packed, *halves)


def merge_kernel(*refs):
    *grad_refs, q_ref, kv_ref = refs
    kv_heads = len(grad_refs)
    span = q_ref.shape[1] // kv_heads
    for g, grad_ref in enumerate(grad_refs):
        q_ref[:, g * span : (g + 1) * span] = grad_ref[:, :span]
        for part in range(2):
            at, start = (part * kv_heads + g) * HEAD_SIZE, span + part * HEAD_SIZE
            kv_ref[:, at : at + HEAD_SIZE] = grad_ref[:, start : start + HEAD_SIZE]


def merge(grads, widths):
    return pl.pallas_call(
        merge_kernel,
        out_shape=[
            jax.ShapeDtypeStruct((grads[0].shape[0], width), grads[0].dtype) for width in widths
        ],
        cost_estimate=cost(1024),
        compiler_params=pltpu.CompilerParams(vmem_limit_bytes=VMEM_LIMIT),
        name="merge",
    )(*grads)


def local(
    fresh_q, current_key_value, held_q, retained_key_value, cotangent, norm_gains, plan, segment_ids
):
    sections, replicas = lax.axis_size("section"), lax.axis_size("dp")
    opposite = [(i, -i % sections) for i in range(sections)]
    up = [(i, (i + 1) % sections) for i in range(sections)]
    down = [(i, (i - 1) % sections) for i in range(sections)]
    segments = segment_ids[0]
    widths = fresh_q.shape[2], current_key_value.shape[2]

    def hop(value, pairs):
        return lax.ppermute(value, "section", pairs)

    numbers = jnp.broadcast_to(plan[0].astype(jnp.float32)[:, None], (2, HEAD_SIZE))
    fresh = hop(jnp.concatenate([fresh_q[0], current_key_value[0]], axis=1), up)
    held = hop(jnp.concatenate([held_q[0], retained_key_value[0]], axis=1), opposite)
    side = hop(jnp.concatenate([norm_gains[0], numbers], axis=0), up)
    stored = hop(fresh, opposite)
    kv_heads = widths[1] // HEAD_SIZE // 2
    near, parts = [], []
    for heads in (range(kv_heads // 2, kv_heads), range(kv_heads // 2)):
        made = [backward(g, kv_heads, held, cotangent[0], side, segments) for g in heads]
        near.append([grad for grad, _ in made])
        parts += [part for _, part in made]
    second, first = (grads[0] if len(grads) == 1 else jnp.concatenate(grads, axis=1) for grads in near)
    gain = functools.reduce(jnp.add, parts)
    fixed = [i for i in range(sections) if -i % sections == i]
    across = [(i, (i + sections // 2) % sections) for i in fixed]
    after = [(j, (i - 1) % sections) for i, j in across]
    straight = [(i, (i - 1) % sections) for i in range(sections) if i not in fixed]
    crossed = hop(first, across)
    me = lax.axis_index("section")
    stays = functools.reduce(jnp.logical_or, [me == i for i in fixed])
    second = hop(second, down)
    step = 1
    while 2 * step < replicas:
        gain = gain + lax.ppermute(gain, "dp", [(i, i ^ step) for i in range(replicas)])
        step *= 2
    crossed, second, gain = lax.optimization_barrier((crossed, second, gain))
    first = jnp.where(stays, crossed, first)
    first = hop(first, after + straight)
    attention_out = forward(fresh, widths[0], side, segments)

    halves = [
        lax.ppermute(
            gain,
            ("section", "dp"),
            [
                (i * replicas + j, (i - 1) % sections * replicas + (j ^ other))
                for i in range(sections)
                for j in range(replicas)
            ],
        )
        for other in (0, step)
    ]
    span = sum(widths) // kv_heads
    grads = [
        whole[:, at : at + span] for whole in (first, second) for at in range(0, whole.shape[1], span)
    ]
    grad_q, grad_kv = merge(grads, widths)
    stored, grad_q = lax.optimization_barrier((stored, grad_q))
    stored_q, stored_kv, gain = unpack(stored, halves, widths, 1.0 / replicas)
    return (
        attention_out[None],
        stored_q[None],
        stored_kv[None],
        grad_q[None],
        grad_kv[None],
        gain[None],
    )


def solution(mesh):
    rows = P("section", "dp", None)
    gains = P("section", None, None)
    return jax.shard_map(
        local,
        mesh=mesh,
        in_specs=(rows, rows, rows, rows, rows, gains, P("section", None), P("dp", None, None)),
        out_specs=(rows, rows, rows, rows, rows, gains),
        check_vma=False,
    )
```

```python
import functools
import math

import jax
import jax.numpy as jnp
from jax import lax
from jax.experimental import pallas as pl
from jax.experimental.pallas import tpu as pltpu
from jax.sharding import PartitionSpec as P

HEAD_SIZE = 128
EPSILON = 1e-06
SCORE_SCALE = 1.0 / math.sqrt(HEAD_SIZE)
EXP2_SCALE = SCORE_SCALE * math.log2(math.e)

VMEM_LIMIT = 16 << 20
CUT_NUM, CUT_DEN = 10, 20
NT = (((1,), (1,)), ((), ()))
TN = (((0,), (0,)), ((), ()))
NN = (((1,), (0,)), ((), ()))


def dot(a, b, dims):
    return lax.dot_general(a, b, dims, preferred_element_type=jnp.float32)


def head(ref, index):
    return ref[:, index * HEAD_SIZE : (index + 1) * HEAD_SIZE]


def stacked(ref, first, count):
    return jnp.concatenate([head(ref, first + i) for i in range(count)], axis=0)


def allowed_pairs(segment_ref, chosen, copies):
    micro, tokens = segment_ref.shape
    ids = segment_ref[...].astype(jnp.float32)
    number = lax.broadcasted_iota(jnp.int32, (micro, tokens), 0).astype(jnp.float32)
    row = jnp.sum(jnp.where(number == chosen[:, :tokens], ids, 0.0), axis=0, keepdims=True)
    keys_at = lax.broadcasted_iota(jnp.int32, (tokens, tokens), 0)
    queries_at = lax.broadcasted_iota(jnp.int32, (tokens, tokens), 1)
    column = jnp.sum(jnp.where(keys_at == queries_at, row, 0.0), axis=1, keepdims=True)
    allowed = ((keys_at <= queries_at) & (column == row)).astype(jnp.float32)
    return jnp.concatenate([allowed] * copies, axis=1) > 0.5


def normalized(values):
    wide = values.astype(jnp.float32)
    factor = lax.rsqrt(jnp.mean(wide * wide, axis=1, keepdims=True) + EPSILON)
    return wide * factor, factor


def probabilities(key, query, allowed):
    scores = dot(key, query, NT)
    weights = jnp.where(allowed, jnp.exp2(scores * EXP2_SCALE), 0.0)
    return weights * (1.0 / jnp.sum(weights, axis=0, keepdims=True))


def forward_kernel(packed_ref, side_ref, segment_ref, out_ref, held_ref, sems):
    side = side_ref[...]
    tokens = packed_ref.shape[0]
    heads = out_ref.shape[1] // HEAD_SIZE
    kv_heads = (packed_ref.shape[1] // HEAD_SIZE - heads) // 2
    per_kv = heads // kv_heads
    allowed = allowed_pairs(segment_ref, side[2:3], per_kv)
    copies = []
    for g in range(kv_heads):
        key_hat, _ = normalized(head(packed_ref, heads + g))
        key = (key_hat * side[1:2]).astype(jnp.bfloat16)
        value = head(packed_ref, heads + kv_heads + g)
        query_hat, _ = normalized(stacked(packed_ref, g * per_kv, per_kv))
        query = (query_hat * side[0:1]).astype(jnp.bfloat16)
        probs = probabilities(key, query, allowed).astype(jnp.bfloat16)
        out = dot(probs, value, TN).astype(jnp.bfloat16)
        for i in range(per_kv):
            h = g * per_kv + i
            held_ref[:, h * HEAD_SIZE : (h + 1) * HEAD_SIZE] = out[i * tokens : (i + 1) * tokens]
        columns = pl.ds(g * per_kv * HEAD_SIZE, per_kv * HEAD_SIZE)
        copies.append(
            pltpu.make_async_copy(held_ref.at[:, columns], out_ref.at[:, columns], sems.at[g])
        )
        copies[-1].start()
    for copy in copies:
        copy.wait()


def norm_back(hat, factor, scaled_gain, d_normed):
    terms = d_normed * hat
    inner = jnp.sum(terms * scaled_gain, axis=1, keepdims=True) * (1.0 / HEAD_SIZE)
    return (d_normed * scaled_gain - hat * inner) * factor, terms


def summed_rows(terms):
    return jnp.sum(terms.reshape(-1, 8, terms.shape[1]), axis=0)


def backward_kernel(packed_ref, up_ref, side_ref, segment_ref, *outs):
    *grad_refs, gain_ref = outs

    def write(block, value):
        first = grad_refs[0].shape[1] // HEAD_SIZE
        ref, at = (grad_refs[0], block) if block < first else (grad_refs[1], block - first)
        ref[:, at * HEAD_SIZE : (at + 1) * HEAD_SIZE] = value.astype(jnp.bfloat16)

    side = side_ref[...]
    tokens = packed_ref.shape[0]
    heads = up_ref.shape[1] // HEAD_SIZE
    kv_heads = (packed_ref.shape[1] // HEAD_SIZE - heads) // 2
    per_kv = heads // kv_heads
    allowed = allowed_pairs(segment_ref, side[3:4], per_kv)
    q_gain, k_gain = side[0:1], side[1:2]
    q_terms = k_terms = 0.0
    for g in range(kv_heads):
        key_hat, key_factor = normalized(head(packed_ref, heads + g))
        key = (key_hat * k_gain).astype(jnp.bfloat16)
        value = head(packed_ref, heads + kv_heads + g)
        query_hat, query_factor = normalized(stacked(packed_ref, g * per_kv, per_kv))
        query = (query_hat * q_gain).astype(jnp.bfloat16)
        upstream = stacked(up_ref, g * per_kv, per_kv)
        probs = probabilities(key, query, allowed)
        d_probs = dot(value, upstream, NT)
        d_value = dot(probs.astype(jnp.bfloat16), upstream, NN)
        centre = jnp.sum(probs * d_probs, axis=0, keepdims=True)
        d_scores = (probs * (d_probs - centre)).astype(jnp.bfloat16)
        d_key = dot(d_scores, query, NN)
        d_query, terms = norm_back(
            query_hat, query_factor, q_gain * SCORE_SCALE, dot(d_scores, key, TN)
        )
        q_terms += summed_rows(terms)
        for i in range(per_kv):
            write(g * per_kv + i, d_query[i * tokens : (i + 1) * tokens])
        d_key, terms = norm_back(key_hat, key_factor, k_gain * SCORE_SCALE, d_key)
        k_terms += summed_rows(terms)
        write(heads + g, d_key)
        write(heads + kv_heads + g, d_value)
    gain_ref[0:1, :] = jnp.sum(q_terms, axis=0, keepdims=True) * SCORE_SCALE
    gain_ref[1:2, :] = jnp.sum(k_terms, axis=0, keepdims=True) * SCORE_SCALE


def cost(work):
    return pl.CostEstimate(flops=work, bytes_accessed=1024, transcendentals=0)


VMEM = pl.BlockSpec(memory_space=pltpu.VMEM)


def forward(fresh, q_width, side, segments):
    tokens, width = fresh.shape
    kv_heads = (width - q_width) // HEAD_SIZE // 2
    return pl.pallas_call(
        forward_kernel,
        out_shape=jax.ShapeDtypeStruct((tokens, q_width), fresh.dtype),
        in_specs=[VMEM] * 3,
        out_specs=pl.BlockSpec(memory_space=pl.ANY),
        scratch_shapes=[
            pltpu.VMEM((tokens, q_width), fresh.dtype),
            pltpu.SemaphoreType.DMA((kv_heads,)),
        ],
        cost_estimate=cost(1024),
        compiler_params=pltpu.CompilerParams(vmem_limit_bytes=VMEM_LIMIT),
        name="forward",
    )(fresh, side, segments)


def backward(packed, upstream, side, segments):
    tokens, width = packed.shape
    cut = width // HEAD_SIZE * CUT_NUM // CUT_DEN * HEAD_SIZE
    return pl.pallas_call(
        backward_kernel,
        out_shape=[jax.ShapeDtypeStruct((tokens, w), packed.dtype) for w in (cut, width - cut)]
        + [jax.ShapeDtypeStruct((2, HEAD_SIZE), jnp.float32)],
        in_specs=[VMEM] * 4,
        out_specs=[VMEM] * 3,
        cost_estimate=cost(1024),
        compiler_params=pltpu.CompilerParams(vmem_limit_bytes=VMEM_LIMIT),
        name="backward",
    )(packed, upstream, side, segments)


def unpack_kernel(share, packed_ref, here_ref, there_ref, q_ref, kv_ref, gain_ref):
    q_width = q_ref.shape[1]
    q_ref[...] = packed_ref[:, :q_width]
    kv_ref[...] = packed_ref[:, q_width : q_width + kv_ref.shape[1]]
    gain_ref[...] = (here_ref[...] + there_ref[...]) * share


def unpack(packed, halves, widths, share):
    shapes = [jax.ShapeDtypeStruct((packed.shape[0], width), packed.dtype) for width in widths]
    return pl.pallas_call(
        functools.partial(unpack_kernel, share),
        out_shape=shapes + [jax.ShapeDtypeStruct(halves[0].shape, halves[0].dtype)],
        cost_estimate=cost(1024),
        compiler_params=pltpu.CompilerParams(vmem_limit_bytes=VMEM_LIMIT),
        name="unpack",
    )(packed, *halves)


def merge_kernel(first_ref, second_ref, q_ref, kv_ref):
    cut, q_width = first_ref.shape[1], q_ref.shape[1]
    q_ref[:, :cut] = first_ref[...]
    q_ref[:, cut:] = second_ref[:, : q_width - cut]
    kv_ref[...] = second_ref[:, q_width - cut :]


def merge(grads, widths):
    return pl.pallas_call(
        merge_kernel,
        out_shape=[
            jax.ShapeDtypeStruct((grads[0].shape[0], width), grads[0].dtype) for width in widths
        ],
        cost_estimate=cost(1024),
        compiler_params=pltpu.CompilerParams(vmem_limit_bytes=VMEM_LIMIT),
        name="merge",
    )(*grads)


def local(
    fresh_q, current_key_value, held_q, retained_key_value, cotangent, norm_gains, plan, segment_ids
):
    sections, replicas = lax.axis_size("section"), lax.axis_size("dp")
    opposite = [(i, -i % sections) for i in range(sections)]
    up = [(i, (i + 1) % sections) for i in range(sections)]
    down = [(i, (i - 1) % sections) for i in range(sections)]
    segments = segment_ids[0]
    widths = fresh_q.shape[2], current_key_value.shape[2]

    def hop(value, pairs):
        return lax.ppermute(value, "section", pairs)

    numbers = jnp.broadcast_to(plan[0].astype(jnp.float32)[:, None], (2, HEAD_SIZE))
    fresh = hop(jnp.concatenate([fresh_q[0], current_key_value[0]], axis=1), up)
    held = hop(jnp.concatenate([held_q[0], retained_key_value[0]], axis=1), opposite)
    side = hop(jnp.concatenate([norm_gains[0], numbers], axis=0), up)
    stored = hop(fresh, opposite)
    first, second, gain = backward(held, cotangent[0], side, segments)
    fixed = [i for i in range(sections) if -i % sections == i]
    across = [(i, (i + sections // 2) % sections) for i in fixed]
    after = [(j, (i - 1) % sections) for i, j in across]
    straight = [(i, (i - 1) % sections) for i in range(sections) if i not in fixed]
    crossed = hop(first, across)
    me = lax.axis_index("section")
    stays = functools.reduce(jnp.logical_or, [me == i for i in fixed])
    second = hop(second, down)
    step = 1
    while 2 * step < replicas:
        gain = gain + lax.ppermute(gain, "dp", [(i, i ^ step) for i in range(replicas)])
        step *= 2
    crossed, second, gain = lax.optimization_barrier((crossed, second, gain))
    first = jnp.where(stays, crossed, first)
    first = hop(first, after + straight)
    attention_out = forward(fresh, widths[0], side, segments)

    halves = [
        lax.ppermute(
            gain,
            ("section", "dp"),
            [
                (i * replicas + j, (i - 1) % sections * replicas + (j ^ other))
                for i in range(sections)
                for j in range(replicas)
            ],
        )
        for other in (0, step)
    ]
    grad_q, grad_kv = merge((first, second), widths)
    stored, grad_q = lax.optimization_barrier((stored, grad_q))
    stored_q, stored_kv, gain = unpack(stored, halves, widths, 1.0 / replicas)
    return (
        attention_out[None],
        stored_q[None],
        stored_kv[None],
        grad_q[None],
        grad_kv[None],
        gain[None],
    )


def solution(mesh):
    rows = P("section", "dp", None)
    gains = P("section", None, None)
    return jax.shard_map(
        local,
        mesh=mesh,
        in_specs=(rows, rows, rows, rows, rows, gains, P("section", None), P("dp", None, None)),
        out_specs=(rows, rows, rows, rows, rows, gains),
        check_vma=False,
    )
```
